128 devices in a mesh: dp: 8 (over z, y_hi), tensor: 16 (over x, y_lo, core).
Axes of the slice: x: 4, y: 4 (y_hi: 2, y_lo: 2; y = y_hi * 2 + y_lo), z: 4, core: 2. Of those that a mesh axis runs over, the one named last changes fastest.
Arguments:
- doc_rows: bfloat16 [1024, 8192], P('tensor', 'dp'), may hold values from -6 to 6
- packed_slot: int32 [1024], P('tensor'), may hold values from 0 to 1023, as said below
- gate_weight: bfloat16 [8192, 28672], P('dp', 'tensor'), may hold values from -0.0625 to 0.0625
- up_weight: bfloat16 [8192, 28672], P('dp', 'tensor'), may hold values from -0.0625 to 0.0625
- down_weight: bfloat16 [28672, 8192], P('tensor', 'dp'), may hold values from -0.03125 to 0.03125
Outputs:
- mixed: bfloat16 [1024, 8192], P('tensor', 'dp')
The draws below stay inside these ranges and needn't reach their ends.
Inputs may be any that keep to these rules, and one draw needn't show every extreme that they name: packed_slot is a permutation of 0 to 1023. Call positions p with p // 64 equal a block. The rows of one index of tensor (aligned runs of 64 rows) put at most 8 rows into one block, and each such run puts exactly 8 rows into some block.
All inputs are finite; a program needn't handle non-finite values.
Results may differ from the reference program's by a relative error of at most 0.02.
Values may be sent and summed in bfloat16 or wider, within the bound.
A program may use at most 128 MiB of HBM per device.

```python
import jax
import jax.numpy as jnp
from jax import lax

D = 8192
FF = 28672
ROWS_DEV = 64
TOKENS = 1024
N_DP = 8


def draw_packed_slot(key, part):
    key = jax.random.fold_in(key, 11)
    row_count = ROWS_DEV
    block_count = TOKENS // ROWS_DEV
    slot_cap = ROWS_DEV // 8
    key_list = jax.random.split(key, 5)
    remain = row_count - slot_cap
    others = jnp.full((block_count - 1,), remain // (block_count - 1), jnp.int32)
    others = others + (jax.random.permutation(key_list[0], block_count - 1) < remain % (block_count - 1)).astype(jnp.int32)
    pair_count = (block_count - 1) // 2
    if pair_count > 0:
        giver = others[0:2 * pair_count:2]
        taker = others[1:2 * pair_count:2]
        limit = jnp.minimum(giver, slot_cap - taker)
        amount = jax.random.randint(key_list[1], (pair_count,), 0, limit + 1)
        others = others.at[0:2 * pair_count:2].add(-amount).at[1:2 * pair_count:2].add(amount)
    counts = jnp.concatenate([jnp.full((1,), slot_cap, jnp.int32), others])
    counts = counts[jax.random.permutation(key_list[2], block_count)]
    shifts = jax.random.permutation(key_list[3], block_count)
    column = jnp.arange(block_count, dtype=jnp.int32)
    matrix = counts[(column[None, :] + shifts[:, None]) % block_count]
    inclusive = jnp.cumsum(matrix, axis=1)
    run_start = inclusive - matrix
    within = jnp.arange(row_count, dtype=jnp.int32)
    target = jnp.sum((inclusive[:, None, :] <= within[None, :, None]).astype(jnp.int32), axis=2)
    in_run = within[None, :] - jnp.take_along_axis(run_start, target, axis=1)
    before = jnp.cumsum(matrix, axis=0) - matrix
    offset = jnp.take_along_axis(before, target, axis=1) + in_run
    perm_keys = jax.random.split(key_list[4], block_count)
    block_perms = jax.vmap(lambda one_key: jax.random.permutation(one_key, row_count))(perm_keys)
    position = target * row_count + block_perms[target, offset]
    return position.reshape(-1).astype(jnp.int32)


def levels(own_key, dims, pieces, smallest, top_value):
    loudness = 1.0
    for dim, shards_of in pieces:
        heights = jax.random.uniform(jax.random.fold_in(jax.random.fold_in(own_key, 6), dim), (shards_of,), jnp.float32, smallest / len(pieces), top_value / len(pieces))
        loudness = loudness * jnp.repeat(jnp.exp(heights), dims[dim] // shards_of).reshape((-1,) + (1,) * (len(dims) - 1 - dim))
    return loudness


def normal_values(stream_key, dims, width, most, shards=(), kind=jnp.bfloat16):
    array = width * jax.random.normal(stream_key, dims, jnp.float32)
    if shards:
        array = array * levels(stream_key, dims, shards, -0.22, 0.18)
    return jnp.clip(array, -most, most).astype(kind)


def setup_inputs(seed: int = 0) -> dict:
    arg_keys = jax.random.split(jax.random.key(seed), 6)
    doc_rows = normal_values(arg_keys[0], (TOKENS, D), 1.0, 6.0, ((0, 16), (1, 8)))
    packed_slot = draw_packed_slot(jax.random.fold_in(arg_keys[5], 71), 0)
    gate_weight = normal_values(arg_keys[2], (D, FF), D ** -0.5, 0.0625, ((0, 8), (1, 16)))
    up_weight = normal_values(arg_keys[3], (D, FF), D ** -0.5, 0.0625, ((0, 8), (1, 16)))
    down_weight = normal_values(arg_keys[4], (FF, D), FF ** -0.5, 0.03125, ((0, 16), (1, 8)))
    return dict(doc_rows=doc_rows, packed_slot=packed_slot, gate_weight=gate_weight, up_weight=up_weight, down_weight=down_weight)


def reference(doc_rows, packed_slot, gate_weight, up_weight, down_weight):
    packed = jnp.zeros_like(doc_rows).at[packed_slot].set(doc_rows)
    block_width = D // N_DP
    gate_sum = jnp.zeros((TOKENS, FF), jnp.float32)
    up_sum = jnp.zeros((TOKENS, FF), jnp.float32)
    for block_index in range(N_DP):
        lower = block_index * block_width
        columns = packed[:, lower:lower + block_width]
        gate_term = jnp.dot(columns, gate_weight[lower:lower + block_width], preferred_element_type=jnp.float32)
        up_term = jnp.dot(columns, up_weight[lower:lower + block_width], preferred_element_type=jnp.float32)
        gate_low = lax.optimization_barrier(gate_term.astype(jnp.bfloat16))
        up_low = lax.optimization_barrier(up_term.astype(jnp.bfloat16))
        gate_sum = gate_sum + gate_low.astype(jnp.float32)
        up_sum = up_sum + up_low.astype(jnp.float32)
    hidden = (jax.nn.silu(gate_sum) * up_sum).astype(jnp.bfloat16)
    update = jnp.dot(hidden, down_weight, preferred_element_type=jnp.float32)
    return (packed.astype(jnp.float32) + update).astype(jnp.bfloat16)
```

```python
import functools

import jax
import jax.numpy as jnp
from jax import lax
from jax.experimental import pallas as pl
from jax.experimental.pallas import tpu as pltpu
from jax.sharding import PartitionSpec as P

MESH = pl.DeviceIdType.MESH
BF16 = jnp.bfloat16
F32 = jnp.float32

NC = 8
TILE = 256
TA = 4
TB = 3
CA = TA * TILE
CB = TB * TILE
HB2 = CB // 2
WIDTH = 1024
ROWS = 64

A_PT, A_PL, A_CB, A_Y = 0, 2, 4, 6
B_Y, B_PT, B_PL, B_CB = 7, 8, 10, 12
GA_Y, GA_Z, GA_F = 14, 15, 17
GB_Z, GB_F, GB_Y = 19, 21, 23
T_C, T_X, X_IN, X_CORE = 24, 25, 26, 27
KINDS = 28


def kernel(
    slot_ref, doc_ref, gate_ref, up_ref, down_ref, out_ref,
    w1, wd, xs_all, pa, pb,
    pt_a, pl_a, cs_a, cr_a, ys_a, yr_a,
    yr_b, q_b, pt_b, pl_b, cs_b, cr_b,
    ha, hb, o2, o2r, xs, xr, acc, ysnd, yrcv,
    snd, got, pos_s, pos_g,
    wsem, dsem, lsem, ssem, rsem, tsend, trecv, psend, precv, gsend, grecv,
):
    dp = lax.axis_index("dp")
    t = lax.axis_index("tensor")
    z, yh = dp // 2, dp % 2
    x, yl, core = t // 4, (t // 2) % 2, t % 2
    zn, zb, z2 = (z + 1) % 4, (z + 3) % 4, (z + 2) % 4
    dev_z = ((zn * 2 + yh, t), (zb * 2 + yh, t))
    dev_y = (z * 2 + 1 - yh, t)
    dev_core = (dp, t + 1 - 2 * core)
    dev_yl = (dp, t + 2 - 4 * yl)
    other = 1 - yh

    def dev_x(k):
        return (dp, ((x + k) % 4) * 4 + t % 4)

    def remote(src, dst, kind, c, device):
        return pltpu.make_async_remote_copy(
            src_ref=src, dst_ref=dst, send_sem=ssem.at[kind], recv_sem=rsem.at[kind, c],
            device_id=device, device_id_type=MESH,
        )

    def arrive(dst, kind, c):
        remote(dst, dst, kind, c, dev_y).wait_recv()

    own_x = xs_all.at[0, pl.ds(core * ROWS, ROWS)]
    doc_load = pltpu.make_async_copy(doc_ref, own_x, lsem)
    doc_load.start()

    def w_load(h, j):
        src = (gate_ref, up_ref)[h].at[:, pl.ds(pl.multiple_of(j * TILE, TILE), TILE)]
        return pltpu.make_async_copy(src, w1.at[h, j], wsem.at[h, j])

    def load_tile(j, carry):
        w_load(0, j).start()
        w_load(1, j).start()
        return carry

    lax.fori_loop(0, TA + TB, load_tile, 0)
    d_load = pltpu.make_async_copy(down_ref, wd, dsem)
    d_load.start()

    barrier = pltpu.get_barrier_semaphore()

    def greet(k, carry):
        pl.semaphore_signal(
            barrier, inc=1, device_id=(dp, (t + k) % 16), device_id_type=MESH
        )
        return carry

    lax.fori_loop(1, 16, greet, 0)
    for device in (dev_z[0], dev_z[1], dev_y):
        pl.semaphore_signal(barrier, inc=1, device_id=device, device_id_type=MESH)
    doc_load.wait()
    pl.semaphore_wait(barrier, 18)

    remote(own_x, own_x, X_CORE, 0, dev_core).start()
    remote(own_x, xs_all.at[1, pl.ds(core * ROWS, ROWS)], X_IN, 1, dev_yl).start()

    def x_slot(k, dy):
        return 2 * k + 1 - dy

    for k in (1, 3, 2):
        c = x_slot(k, 0)
        remote(own_x, xs_all.at[c, pl.ds(core * ROWS, ROWS)], X_IN, c, dev_x(4 - k)).start()

    def plan():
        slots = slot_ref[...]
        block = lax.shift_right_logical(slots, 6)
        place = slots & 63
        blocks = lax.broadcasted_iota(jnp.int32, (16, ROWS), 0)
        hot = jnp.where(blocks == block, 1.0, 0.0)
        before = jnp.where(
            lax.broadcasted_iota(jnp.int32, (ROWS, ROWS), 0)
            < lax.broadcasted_iota(jnp.int32, (ROWS, ROWS), 1),
            1.0,
            0.0,
        )
        count = jnp.dot(hot.astype(BF16), before.astype(BF16), preferred_element_type=F32)
        rank = jnp.sum(hot * count, axis=0, keepdims=True).astype(jnp.int32)
        return block, rank, place

    def placed(half):
        block, rank, _ = plan()
        q = lax.broadcasted_iota(jnp.int32, (256, ROWS), 0)
        return (block * 16 + half * 8 + rank) == q

    def send_places():
        _, _, place = plan()
        pick = placed(0) | placed(1)
        pos = jnp.sum(jnp.where(pick, place + 1, 0), axis=1, keepdims=True) - 1
        pos_s[...] = jnp.broadcast_to(pos, (256, 128))

        def one(k, carry):
            peer = (t + k) % 16
            place_copy(k, peer).start()
            return carry

        lax.fori_loop(1, 16, one, 0)
        pos_g[pl.ds(t * 16, 16)] = pos_s[pl.ds(t * 16, 16)]

    def place_copy(k, peer):
        return pltpu.make_async_remote_copy(
            src_ref=pos_s.at[pl.ds(peer * 16, 16)], dst_ref=pos_g.at[pl.ds(t * 16, 16)],
            send_sem=psend.at[k - 1], recv_sem=precv.at[k - 1], device_id=(dp, peer), device_id_type=MESH,
        )

    def place_arrive(k):
        rows = pos_g.at[pl.ds(((t + 16 - k) % 16) * 16, 16)]
        pltpu.make_async_remote_copy(
            src_ref=rows, dst_ref=rows, send_sem=psend.at[k - 1], recv_sem=precv.at[k - 1],
            device_id=dev_y, device_id_type=MESH,
        ).wait_recv()

    def row_copy(k, peer):
        return pltpu.make_async_remote_copy(
            src_ref=snd.at[pl.ds(peer * 16, 16)], dst_ref=got.at[pl.ds(t * 16, 16)],
            send_sem=gsend.at[k - 1], recv_sem=grecv.at[k - 1], device_id=(dp, peer), device_id_type=MESH,
        )

    def row_arrive(k):
        rows = got.at[pl.ds(((t + 16 - k) % 16) * 16, 16)]
        pltpu.make_async_remote_copy(
            src_ref=rows, dst_ref=rows, send_sem=gsend.at[k - 1], recv_sem=grecv.at[k - 1],
            device_id=dev_y, device_id_type=MESH,
        ).wait_recv()

    def stage0(c):
        arrive(xs_all.at[c, pl.ds((1 - core) * ROWS, ROWS)], X_CORE, c)

        def tile(j, dst, col):
            for h in range(2):
                @pl.when(c == 0)
                def _():
                    w_load(h, j).wait()

                r = jnp.dot(xs_all[c], w1[h, j], preferred_element_type=F32)
                dst[c, h, :, :, :, pl.ds(pl.multiple_of(col, TILE), TILE)] = r.astype(BF16).reshape(2, 4, 16, TILE)

        def tile_b(j, carry):
            tile(TA + j, pb, j * TILE)
            return carry

        def tile_a(j, carry):
            tile(j, pa, j * TILE)
            return carry

        lax.fori_loop(0, TA, tile_a, 0)
        for d in range(2):
            remote(pa.at[c, d, :, z2], pt_a.at[c, d], A_PT + d, c, dev_z[d]).start()
        for d in range(2):
            near = (zn, zb)[d]
            remote(pa.at[c, 1 - d, :, near], pl_a.at[c, d], A_PL + d, c, dev_z[d]).start()
        lax.fori_loop(0, TB, tile_b, 0)
        remote(pb.at[c, :, other], yr_b.at[c], B_Y, c, dev_y).start()

    def next_rows(c):
        rows = xs_all.at[c, pl.ds(core * ROWS, ROWS)]
        arrive(rows, X_IN, c)
        remote(rows, rows, X_CORE, c, dev_core).start()

        @pl.when(c == 1)
        def _():
            for k in (1, 3, 2):
                far = x_slot(k, 1)
                remote(rows, xs_all.at[far, pl.ds(core * ROWS, ROWS)], X_IN, far, dev_x(4 - k)).start()

    def stage1(c):
        for d in range(2):
            near = (zn, zb)[d]
            arrive(pt_a.at[c, d], A_PT + d, c)
            cs_a[c, d] = (pa[c, d, :, near].astype(F32) + pt_a[c, d].astype(F32)).astype(BF16)
            remote(cs_a.at[c, d], cr_a.at[c, d], A_CB + d, c, dev_z[d]).start()
        arrive(yr_b.at[c], B_Y, c)
        q_b[c] = (pb[c, :, yh].astype(F32) + yr_b[c].astype(F32)).astype(BF16)
        for d in range(2):
            remote(q_b.at[c, d, z2], pt_b.at[c, d], B_PT + d, c, dev_z[d]).start()
        for d in range(2):
            near = (zn, zb)[d]
            remote(q_b.at[c, 1 - d, near], pl_b.at[c, d], B_PL + d, c, dev_z[d]).start()

    def z_sum_a(c, h, y):
        return (
            pa[c, h, y, z].astype(F32)
            + cr_a[c, h, y].astype(F32)
            + pl_a[c, 1 - h, y].astype(F32)
        )

    def stage2(c):
        for d in range(2):
            near = (zn, zb)[d]
            arrive(pt_b.at[c, d], B_PT + d, c)
            cs_b[c, d] = (q_b[c, d, near].astype(F32) + pt_b[c, d].astype(F32)).astype(BF16)
            remote(cs_b.at[c, d], cr_b.at[c, d], B_CB + d, c, dev_z[d]).start()
        for d in range(2):
            arrive(pl_a.at[c, d], A_PL + d, c)
            arrive(cr_a.at[c, d], A_CB + d, c)
        for h in range(2):
            ys_a[c, h] = z_sum_a(c, h, other).astype(BF16)
        remote(ys_a.at[c], yr_a.at[c], A_Y, c, dev_y).start()

    def gated(g, u):
        return (g / (1.0 + jnp.exp(-g)) * u).astype(BF16)

    def stage3(c):
        for d in range(2):
            arrive(pl_b.at[c, d], B_PL + d, c)
            arrive(cr_b.at[c, d], B_CB + d, c)
        g, u = (
            q_b[c, h, z].astype(F32) + cr_b[c, h].astype(F32) + pl_b[c, 1 - h].astype(F32)
            for h in range(2)
        )
        hb[c, yh, z] = gated(g, u)
        for d in range(2):
            remote(hb.at[c, yh, z], hb.at[c, yh, z], GB_Z + d, c, dev_z[d]).start()
        arrive(yr_a.at[c], A_Y, c)
        g, u = (z_sum_a(c, h, yh) + yr_a[c, h].astype(F32) for h in range(2))
        ha[c, yh, z] = gated(g, u)
        remote(ha.at[c, yh, z], ha.at[c, yh, z], GA_Y, c, dev_y).start()

    def stage4(c):
        for d in range(2):
            back = (zb, zn)[d]
            arrive(hb.at[c, yh, back], GB_Z + d, c)
            part = hb.at[c, yh, back, :, pl.ds(d * HB2, HB2)]
            remote(part, part, GB_F + d, c, dev_z[d]).start()
        arrive(ha.at[c, other, z], GA_Y, c)
        for d in range(2):
            remote(ha.at[c, :, z], ha.at[c, :, z], GA_Z + d, c, dev_z[d]).start()

    def stage5(c):
        for d in range(2):
            arrive(hb.at[c, yh, z2, :, pl.ds(d * HB2, HB2)], GB_F + d, c)
        remote(hb.at[c, yh], hb.at[c, yh], GB_Y, c, dev_y).start()
        for d in range(2):
            back = (zb, zn)[d]
            arrive(ha.at[c, :, back], GA_Z + d, c)
            part = ha.at[c, d, back]
            remote(part, part, GA_F + d, c, dev_z[d]).start()

    def stage6(c):
        for d in range(2):
            arrive(ha.at[c, d, z2], GA_F + d, c)
        arrive(hb.at[c, other], GB_Y, c)

        @pl.when(c == 0)
        def _():
            d_load.wait()

        def tile(n, carry):
            cols = pl.ds(pl.multiple_of(n * TILE, TILE), TILE)
            r = jnp.dot(ha[c].reshape(128, CA), wd[0:CA, cols], preferred_element_type=F32)
            r += jnp.dot(hb[c].reshape(128, CB), wd[CA : CA + CB, cols], preferred_element_type=F32)
            o2[c, :, :, cols] = r.astype(BF16).reshape(2, ROWS, TILE)
            return carry

        lax.fori_loop(0, WIDTH // TILE, tile, 0)
        remote(o2.at[c, 1 - core], o2r.at[c], T_C, c, dev_core).start()

    def stage7(c):
        arrive(o2r.at[c], T_C, c)

        @pl.when(c < 2)
        def _():
            acc[c] = o2[c, core].astype(F32) + o2r[c].astype(F32)

        @pl.when(c >= 2)
        def _():
            xs[c] = (o2[c, core].astype(F32) + o2r[c].astype(F32)).astype(BF16)
            remote(xs.at[c], xr.at[c], T_X, c, dev_x(c // 2)).start()

    def yl_copy():
        return pltpu.make_async_remote_copy(
            src_ref=ysnd, dst_ref=yrcv, send_sem=tsend, recv_sem=trecv, device_id=dev_yl, device_id_type=MESH
        )

    def stage8(c):
        dy = (c + 1) % 2
        arrive(xr.at[c], T_X, c)
        acc[dy] = acc[dy] + xr[c].astype(F32)

        @pl.when(c == NC - 2)
        def _():
            ysnd[...] = acc[1].astype(BF16)
            yl_copy().start()

    stages = (stage0, stage1, stage2, stage3, stage4, stage5, stage6, stage7, stage8)

    def step(s, carry):
        for j, stage in enumerate(stages):
            c = s - j
            low = 2 if stage is stage8 else 0
            pl.when((c >= low) & (c < NC))(functools.partial(stage, c))
            if j == 0:

                @pl.when(s == 0)
                def _():
                    send_places()

                @pl.when(s < NC - 1)
                def _():
                    next_rows(s + 1)

        return carry

    lax.fori_loop(0, NC + len(stages) - 1, step, 0)

    yl_copy().wait_recv()
    rows = (
        xs_all[0, pl.ds(core * ROWS, ROWS)].astype(F32)
        + acc[0]
        + yrcv[...].astype(F32)
    ).astype(BF16)
    half = WIDTH // 2
    packed = jnp.dot(
        jnp.where(placed(0), 1.0, 0.0).astype(BF16), rows[:, :half], preferred_element_type=F32
    ) + jnp.dot(
        jnp.where(placed(1), 1.0, 0.0).astype(BF16), rows[:, half:], preferred_element_type=F32
    )
    snd[...] = packed.astype(BF16)

    def start_rows(k, carry):
        row_copy(k, (t + k) % 16).start()
        return carry

    lax.fori_loop(1, 16, start_rows, 0)
    got[pl.ds(t * 16, 16)] = snd[pl.ds(t * 16, 16)]

    def wait_places(k, carry):
        place_arrive(k)
        return carry

    lax.fori_loop(1, 16, wait_places, 0)
    slot_of = pos_g[:, 0:ROWS]
    q = lax.broadcasted_iota(jnp.int32, (256, ROWS), 0)
    here = slot_of == lax.broadcasted_iota(jnp.int32, (256, ROWS), 1)

    def wait_rows(k, carry):
        row_arrive(k)
        return carry

    lax.fori_loop(1, 16, wait_rows, 0)
    for part in range(2):
        pick = jnp.where(here & ((q // 8) % 2 == part), 1.0, 0.0).astype(BF16)
        out = lax.dot_general(
            pick, got[...], (((0,), (0,)), ((), ())), preferred_element_type=F32
        )
        out_ref[:, part * half : (part + 1) * half] = out.astype(BF16)

    def sent(ref, sem):
        pltpu.make_async_copy(ref, ref, sem).wait()

    for d in range(2):
        sent(pt_a.at[:, d], ssem.at[A_PT + d])
        sent(pl_a.at[:, d], ssem.at[A_PL + d])
        sent(cr_a.at[:, d], ssem.at[A_CB + d])
        sent(pt_b.at[:, d], ssem.at[B_PT + d])
        sent(pl_b.at[:, d], ssem.at[B_PL + d])
        sent(cr_b.at[:, d], ssem.at[B_CB + d])
        sent(ha.at[:, :, 0], ssem.at[GA_Z + d])
        sent(ha.at[:, 0, 0], ssem.at[GA_F + d])
        sent(hb.at[:, 0, 0], ssem.at[GB_Z + d])
        sent(hb.at[:, 0, 0, :, pl.ds(0, HB2)], ssem.at[GB_F + d])
    sent(yr_a, ssem.at[A_Y])
    sent(yr_b, ssem.at[B_Y])
    sent(ha.at[:, 0, 0], ssem.at[GA_Y])
    sent(hb.at[:, 0], ssem.at[GB_Y])
    sent(o2r, ssem.at[T_C])
    sent(xr.at[pl.ds(2, NC - 2)], ssem.at[T_X])
    sent(xs_all.at[:, pl.ds(0, ROWS)], ssem.at[X_CORE])
    sent(xs_all.at[pl.ds(1, NC - 1), pl.ds(0, ROWS)], ssem.at[X_IN])
    yl_copy().wait_send()

    def wait_sent(k, carry):
        peer = (t + k) % 16
        place_copy(k, peer).wait_send()
        row_copy(k, peer).wait_send()
        return carry

    lax.fori_loop(1, 16, wait_sent, 0)


def local(doc_rows, packed_slot, gate_weight, up_weight, down_weight):
    anywhere = pl.BlockSpec(memory_space=pl.ANY)
    vmem = pl.BlockSpec(memory_space=pltpu.VMEM)

    def buf(*shape, dtype=BF16):
        return pltpu.VMEM(shape, dtype)

    dma = pltpu.SemaphoreType.DMA
    return pl.pallas_call(
        kernel,
        out_shape=jax.ShapeDtypeStruct((ROWS, WIDTH), BF16),
        in_specs=[vmem, anywhere, anywhere, anywhere, anywhere],
        out_specs=vmem,
        scratch_shapes=[
            buf(2, TA + TB, WIDTH, TILE),
            buf(CA + CB, WIDTH),
            buf(NC, 128, WIDTH),
            buf(NC, 2, 2, 4, 16, CA),
            buf(NC, 2, 2, 4, 16, CB),
            buf(NC, 2, 2, 16, CA),
            buf(NC, 2, 2, 16, CA),
            buf(NC, 2, 2, 16, CA),
            buf(NC, 2, 2, 16, CA),
            buf(NC, 2, 16, CA),
            buf(NC, 2, 16, CA),
            buf(NC, 2, 4, 16, CB),
            buf(NC, 2, 4, 16, CB),
            buf(NC, 2, 16, CB),
            buf(NC, 2, 16, CB),
            buf(NC, 2, 16, CB),
            buf(NC, 2, 16, CB),
            buf(NC, 2, 4, 16, CA),
            buf(NC, 2, 4, 16, CB),
            buf(NC, 2, ROWS, WIDTH),
            buf(NC, ROWS, WIDTH),
            buf(NC, ROWS, WIDTH),
            buf(NC, ROWS, WIDTH),
            buf(2, ROWS, WIDTH, dtype=F32),
            buf(ROWS, WIDTH),
            buf(ROWS, WIDTH),
            buf(256, WIDTH // 2),
            buf(256, WIDTH // 2),
            buf(256, 128, dtype=jnp.int32),
            buf(256, 128, dtype=jnp.int32),
            dma((2, TA + TB)),
            dma,
            dma,
            dma((KINDS,)),
            dma((KINDS, NC)),
            dma,
            dma,
            dma((15,)),
            dma((15,)),
            dma((15,)),
            dma((15,)),
        ],
        compiler_params=pltpu.CompilerParams(
            collective_id=0, has_side_effects=True, vmem_limit_bytes=60 << 20
        ),
        cost_estimate=pl.CostEstimate(
            flops=2 * 1024 * 1024 * 5376, bytes_accessed=12 << 20, transcendentals=1024 * 1792 // 8
        ),
        name="layer",
    )(packed_slot.reshape(1, ROWS), doc_rows, gate_weight, up_weight, down_weight)


def solution(mesh):
    return jax.shard_map(
        local,
        mesh=mesh,
        in_specs=(
            P("tensor", "dp"),
            P("tensor"),
            P("dp", "tensor"),
            P("dp", "tensor"),
            P("tensor", "dp"),
        ),
        out_specs=P("tensor", "dp"),
        check_vma=False,
    )
```

```python
import jax
import jax.numpy as jnp
from jax import lax
from jax.experimental import pallas as pl
from jax.experimental.pallas import tpu as pltpu
from jax.sharding import PartitionSpec as P

MESH = pl.DeviceIdType.MESH
BF16 = jnp.bfloat16
F32 = jnp.float32

NC = 8
TILE = 256
TA = 4
TB = 3
CA = TA * TILE
CB = TB * TILE
HB2 = CB // 2
WIDTH = 1024
ROWS = 64

A_PT, A_PL, A_CB, A_Y = 0, 2, 4, 6
B_Y, B_PT, B_PL, B_CB = 7, 8, 10, 12
GA_Y, GA_Z, GA_F = 14, 15, 17
GB_Z, GB_F, GB_Y = 19, 21, 23
T_C, T_X, X_IN, X_CORE = 24, 25, 26, 27
KINDS = 28


ORDER = (
    0, 8, 19, 24, 17, 3, 23, 11, 7, 15, 21, 5, 13, 20, 31, 27, 136, 48, 29, 35,
    18, 39, 4, 12, 53, 22, 2, 43, 37, 10, 55, 6, 36, 59, 45, 28, 26, 69, 51, 14,
    1, 47, 44, 75, 9, 61, 34, 85, 52, 25, 42, 67, 77, 91, 60, 30, 101, 50, 38, 32,
    68, 58, 93, 76, 71, 83, 54, 40, 46, 33, 66, 74, 84, 49, 99, 109, 137, 92, 70, 62,
    63, 64, 41, 117, 82, 65, 100, 107, 90, 79, 87, 78, 57, 98, 115, 86, 108, 95, 56, 94,
    116, 103, 73, 81, 106, 102, 114, 72, 80, 111, 89, 97, 124, 119, 88, 110, 96, 118, 105, 125,
    122, 123, 104, 127, 113, 112, 126, 128,
)


def kernel(
    slot_ref, doc_ref, gate_ref, up_ref, down_ref, out_ref,
    w1, wd, xs_all, pa, pb,
    pt_a, pl_a, cs_a, cr_a, ys_a, yr_a,
    yr_b, q_b, pt_b, pl_b, cs_b, cr_b,
    ha, hb, o2, o2r, xs, xr, acc, ysnd, yrcv,
    snd, got, pos_s, pos_g, pick_s, pick_r,
    wsem, dsem, lsem, ssem, rsem, tsend, trecv, psend, precv, gsend, grecv,
):
    dp = lax.axis_index("dp")
    t = lax.axis_index("tensor")
    z, yh = dp // 2, dp % 2
    x, yl, core = t // 4, (t // 2) % 2, t % 2
    zn, zb, z2 = (z + 1) % 4, (z + 3) % 4, (z + 2) % 4
    dev_z = ((zn * 2 + yh, t), (zb * 2 + yh, t))
    dev_y = (z * 2 + 1 - yh, t)
    dev_core = (dp, t + 1 - 2 * core)
    dev_yl = (dp, t + 2 - 4 * yl)
    other = 1 - yh

    def dev_x(k):
        return (dp, ((x + k) % 4) * 4 + t % 4)

    def remote(src, dst, kind, c, device):
        return pltpu.make_async_remote_copy(
            src_ref=src, dst_ref=dst, send_sem=ssem.at[kind], recv_sem=rsem.at[kind, c],
            device_id=device, device_id_type=MESH,
        )

    def arrive(dst, kind, c):
        remote(dst, dst, kind, c, dev_y).wait_recv()

    own_x = xs_all.at[0, pl.ds(core * ROWS, ROWS)]
    doc_load = pltpu.make_async_copy(doc_ref, own_x, lsem)
    doc_load.start()

    def w_load(h, j):
        src = (gate_ref, up_ref)[h].at[:, pl.ds(pl.multiple_of(j * TILE, TILE), TILE)]
        return pltpu.make_async_copy(src, w1.at[h, j], wsem.at[h, j])

    def load_tile(j, carry):
        w_load(0, j).start()
        w_load(1, j).start()
        return carry

    lax.fori_loop(0, TA + TB, load_tile, 0)
    d_load = pltpu.make_async_copy(down_ref, wd, dsem)
    d_load.start()

    barrier = pltpu.get_barrier_semaphore()

    def greet(k, carry):
        pl.semaphore_signal(
            barrier, inc=1, device_id=(dp, (t + k) % 16), device_id_type=MESH
        )
        return carry

    lax.fori_loop(1, 16, greet, 0)
    for device in (dev_z[0], dev_z[1], dev_y):
        pl.semaphore_signal(barrier, inc=1, device_id=device, device_id_type=MESH)
    doc_load.wait()
    pl.semaphore_wait(barrier, 18)

    remote(own_x, own_x, X_CORE, 0, dev_core).start()
    remote(own_x, xs_all.at[1, pl.ds(core * ROWS, ROWS)], X_IN, 1, dev_yl).start()

    def x_slot(k, dy):
        return 2 * k + 1 - dy

    for k in (1, 3, 2):
        c = x_slot(k, 0)
        remote(own_x, xs_all.at[c, pl.ds(core * ROWS, ROWS)], X_IN, c, dev_x(4 - k)).start()

    def plan():
        slots = slot_ref[...]
        block = lax.shift_right_logical(slots, 6)
        place = slots & 63
        blocks = lax.broadcasted_iota(jnp.int32, (16, ROWS), 0)
        hot = jnp.where(blocks == block, 1.0, 0.0)
        before = jnp.where(
            lax.broadcasted_iota(jnp.int32, (ROWS, ROWS), 0)
            < lax.broadcasted_iota(jnp.int32, (ROWS, ROWS), 1),
            1.0,
            0.0,
        )
        count = jnp.dot(hot.astype(BF16), before.astype(BF16), preferred_element_type=F32)
        rank = jnp.sum(hot * count, axis=0, keepdims=True).astype(jnp.int32)
        return block, rank, place

    def send_places():
        block, rank, place = plan()
        q = lax.broadcasted_iota(jnp.int32, (256, ROWS), 0)
        home = block * 16 + rank
        pos = 0
        for half in range(2):
            pick = home + half * 8 == q
            pick_s[half] = jnp.where(pick, 1.0, 0.0).astype(BF16)
            pos += jnp.sum(jnp.where(pick, place + 1, 0), axis=1, keepdims=True)
        pos_s[...] = jnp.broadcast_to(pos - 1, (256, 128))

        def one(k, carry):
            place_copy(k, (t + k) % 16).start()
            return carry

        lax.fori_loop(1, 16, one, 0)
        pos_g[pl.ds(t * 16, 16)] = pos_s[pl.ds(t * 16, 16)]

    def take_places():
        def one(k, carry):
            place_arrive(k)
            return carry

        lax.fori_loop(1, 16, one, 0)
        q = lax.broadcasted_iota(jnp.int32, (256, ROWS), 0)
        here = pos_g[:, 0:ROWS] == lax.broadcasted_iota(jnp.int32, (256, ROWS), 1)
        for half in range(2):
            pick_r[half] = jnp.where(here & ((q // 8) % 2 == half), 1.0, 0.0).astype(BF16)

    def place_copy(k, peer):
        return pltpu.make_async_remote_copy(
            src_ref=pos_s.at[pl.ds(peer * 16, 16)], dst_ref=pos_g.at[pl.ds(t * 16, 16)],
            send_sem=psend.at[k - 1], recv_sem=precv.at[k - 1], device_id=(dp, peer), device_id_type=MESH,
        )

    def place_arrive(k):
        rows = pos_g.at[pl.ds(((t + 16 - k) % 16) * 16, 16)]
        pltpu.make_async_remote_copy(
            src_ref=rows, dst_ref=rows, send_sem=psend.at[k - 1], recv_sem=precv.at[k - 1],
            device_id=dev_y, device_id_type=MESH,
        ).wait_recv()

    def row_copy(k, peer):
        return pltpu.make_async_remote_copy(
            src_ref=snd.at[pl.ds(peer * 16, 16)], dst_ref=got.at[pl.ds(t * 16, 16)],
            send_sem=gsend.at[k - 1], recv_sem=grecv.at[k - 1], device_id=(dp, peer), device_id_type=MESH,
        )

    def row_arrive(k):
        rows = got.at[pl.ds(((t + 16 - k) % 16) * 16, 16)]
        pltpu.make_async_remote_copy(
            src_ref=rows, dst_ref=rows, send_sem=gsend.at[k - 1], recv_sem=grecv.at[k - 1],
            device_id=dev_y, device_id_type=MESH,
        ).wait_recv()

    first = set()

    def once(name):
        new = name not in first
        first.add(name)
        return new

    def gate_up(c, dst, base, count):
        fresh = once(base)

        def tile(j, carry):
            for h in range(2):
                if fresh:
                    w_load(h, base + j).wait()
                r = jnp.dot(xs_all[c], w1[h, base + j], preferred_element_type=F32)
                cols = pl.ds(pl.multiple_of(j * TILE, TILE), TILE)
                dst[c, h, :, :, :, cols] = r.astype(BF16).reshape(2, 4, 16, TILE)
            return carry

        lax.fori_loop(0, count, tile, 0)

    def step_0a(c):
        arrive(xs_all.at[c, pl.ds((1 - core) * ROWS, ROWS)], X_CORE, c)
        gate_up(c, pa, 0, TA)
        for d in range(2):
            remote(pa.at[c, d, :, z2], pt_a.at[c, d], A_PT + d, c, dev_z[d]).start()
        for d in range(2):
            near = (zn, zb)[d]
            remote(pa.at[c, 1 - d, :, near], pl_a.at[c, d], A_PL + d, c, dev_z[d]).start()

    def step_0b(c):
        gate_up(c, pb, TA, TB)
        remote(pb.at[c, :, other], yr_b.at[c], B_Y, c, dev_y).start()

    def next_rows(c):
        rows = xs_all.at[c, pl.ds(core * ROWS, ROWS)]
        arrive(rows, X_IN, c)
        remote(rows, rows, X_CORE, c, dev_core).start()
        if c == 1:
            for k in (1, 3, 2):
                far = x_slot(k, 1)
                remote(rows, xs_all.at[far, pl.ds(core * ROWS, ROWS)], X_IN, far, dev_x(4 - k)).start()

    def step_1a(c):
        for d in range(2):
            near = (zn, zb)[d]
            arrive(pt_a.at[c, d], A_PT + d, c)
            cs_a[c, d] = (pa[c, d, :, near].astype(F32) + pt_a[c, d].astype(F32)).astype(BF16)
            remote(cs_a.at[c, d], cr_a.at[c, d], A_CB + d, c, dev_z[d]).start()

    def step_1b(c):
        arrive(yr_b.at[c], B_Y, c)
        q_b[c] = (pb[c, :, yh].astype(F32) + yr_b[c].astype(F32)).astype(BF16)
        for d in range(2):
            remote(q_b.at[c, d, z2], pt_b.at[c, d], B_PT + d, c, dev_z[d]).start()
        for d in range(2):
            near = (zn, zb)[d]
            remote(q_b.at[c, 1 - d, near], pl_b.at[c, d], B_PL + d, c, dev_z[d]).start()

    def z_sum_a(c, h, y):
        return (
            pa[c, h, y, z].astype(F32)
            + cr_a[c, h, y].astype(F32)
            + pl_a[c, 1 - h, y].astype(F32)
        )

    def step_2b(c):
        for d in range(2):
            near = (zn, zb)[d]
            arrive(pt_b.at[c, d], B_PT + d, c)
            cs_b[c, d] = (q_b[c, d, near].astype(F32) + pt_b[c, d].astype(F32)).astype(BF16)
            remote(cs_b.at[c, d], cr_b.at[c, d], B_CB + d, c, dev_z[d]).start()

    def step_2a(c):
        for d in range(2):
            arrive(pl_a.at[c, d], A_PL + d, c)
            arrive(cr_a.at[c, d], A_CB + d, c)
        for h in range(2):
            ys_a[c, h] = z_sum_a(c, h, other).astype(BF16)
        remote(ys_a.at[c], yr_a.at[c], A_Y, c, dev_y).start()

    def gated(g, u):
        return (g / (1.0 + jnp.exp(-g)) * u).astype(BF16)

    def step_3b(c):
        for d in range(2):
            arrive(pl_b.at[c, d], B_PL + d, c)
            arrive(cr_b.at[c, d], B_CB + d, c)
        g, u = (
            q_b[c, h, z].astype(F32) + cr_b[c, h].astype(F32) + pl_b[c, 1 - h].astype(F32)
            for h in range(2)
        )
        hb[c, yh, z] = gated(g, u)
        for d in range(2):
            remote(hb.at[c, yh, z], hb.at[c, yh, z], GB_Z + d, c, dev_z[d]).start()

    def step_3a(c):
        arrive(yr_a.at[c], A_Y, c)
        g, u = (z_sum_a(c, h, yh) + yr_a[c, h].astype(F32) for h in range(2))
        ha[c, yh, z] = gated(g, u)
        remote(ha.at[c, yh, z], ha.at[c, yh, z], GA_Y, c, dev_y).start()

    def step_4b(c):
        for d in range(2):
            back = (zb, zn)[d]
            arrive(hb.at[c, yh, back], GB_Z + d, c)
            part = hb.at[c, yh, back, :, pl.ds(d * HB2, HB2)]
            remote(part, part, GB_F + d, c, dev_z[d]).start()

    def step_4a(c):
        arrive(ha.at[c, other, z], GA_Y, c)
        for d in range(2):
            remote(ha.at[c, :, z], ha.at[c, :, z], GA_Z + d, c, dev_z[d]).start()

    def step_5b(c):
        for d in range(2):
            arrive(hb.at[c, yh, z2, :, pl.ds(d * HB2, HB2)], GB_F + d, c)
        remote(hb.at[c, yh], hb.at[c, yh], GB_Y, c, dev_y).start()

    def step_5a(c):
        for d in range(2):
            back = (zb, zn)[d]
            arrive(ha.at[c, :, back], GA_Z + d, c)
            part = ha.at[c, d, back]
            remote(part, part, GA_F + d, c, dev_z[d]).start()

    def step_6(c):
        for d in range(2):
            arrive(ha.at[c, d, z2], GA_F + d, c)
        arrive(hb.at[c, other], GB_Y, c)
        if once("down"):
            d_load.wait()

        def tile(n, carry):
            cols = pl.ds(pl.multiple_of(n * TILE, TILE), TILE)
            r = jnp.dot(ha[c].reshape(128, CA), wd[0:CA, cols], preferred_element_type=F32)
            r += jnp.dot(hb[c].reshape(128, CB), wd[CA : CA + CB, cols], preferred_element_type=F32)
            o2[c, :, :, cols] = r.astype(BF16).reshape(2, ROWS, TILE)
            return carry

        lax.fori_loop(0, WIDTH // TILE, tile, 0)
        remote(o2.at[c, 1 - core], o2r.at[c], T_C, c, dev_core).start()

    def add(dy, value):
        acc[dy] = value if once(("acc", dy)) else acc[dy] + value

    def step_7(c):
        arrive(o2r.at[c], T_C, c)
        total = o2[c, core].astype(F32) + o2r[c].astype(F32)
        if c < 2:
            add(c, total)
        else:
            xs[c] = total.astype(BF16)
            remote(xs.at[c], xr.at[c], T_X, c, dev_x(c // 2)).start()

    def step_8(c):
        arrive(xr.at[c], T_X, c)
        add((c + 1) % 2, xr[c].astype(F32))

    def yl_copy():
        return pltpu.make_async_remote_copy(
            src_ref=ysnd, dst_ref=yrcv, send_sem=tsend, recv_sem=trecv, device_id=dev_yl, device_id_type=MESH
        )

    def step_y(c):
        ysnd[...] = acc[1].astype(BF16)
        yl_copy().start()

    def step_p(c):
        send_places() if c == 0 else take_places()

    steps = (
        step_0a, step_0b, next_rows, step_1a, step_1b, step_2b, step_2a, step_3b, step_3a,
        step_4b, step_4a, step_5b, step_5a, step_6, step_7, step_8, step_y, step_p,
    )
    for entry in ORDER:
        steps[entry // 8](entry % 8)

    yl_copy().wait_recv()
    rows = (
        xs_all[0, pl.ds(core * ROWS, ROWS)].astype(F32)
        + acc[0]
        + yrcv[...].astype(F32)
    ).astype(BF16)
    half = WIDTH // 2
    packed = jnp.dot(pick_s[0], rows[:, :half], preferred_element_type=F32)
    packed += jnp.dot(pick_s[1], rows[:, half:], preferred_element_type=F32)
    snd[...] = packed.astype(BF16)

    def start_rows(k, carry):
        row_copy(k, (t + k) % 16).start()
        return carry

    lax.fori_loop(1, 16, start_rows, 0)
    got[pl.ds(t * 16, 16)] = snd[pl.ds(t * 16, 16)]

    def sent(ref, sem):
        pltpu.make_async_copy(ref, ref, sem).wait()

    for d in range(2):
        sent(pt_a.at[:, d], ssem.at[A_PT + d])
        sent(pl_a.at[:, d], ssem.at[A_PL + d])
        sent(cr_a.at[:, d], ssem.at[A_CB + d])
        sent(pt_b.at[:, d], ssem.at[B_PT + d])
        sent(pl_b.at[:, d], ssem.at[B_PL + d])
        sent(cr_b.at[:, d], ssem.at[B_CB + d])
        sent(ha.at[:, :, 0], ssem.at[GA_Z + d])
        sent(ha.at[:, 0, 0], ssem.at[GA_F + d])
        sent(hb.at[:, 0, 0], ssem.at[GB_Z + d])
        sent(hb.at[:, 0, 0, :, pl.ds(0, HB2)], ssem.at[GB_F + d])
    sent(yr_a, ssem.at[A_Y])
    sent(yr_b, ssem.at[B_Y])
    sent(ha.at[:, 0, 0], ssem.at[GA_Y])
    sent(hb.at[:, 0], ssem.at[GB_Y])
    sent(o2r, ssem.at[T_C])
    sent(xr.at[pl.ds(2, NC - 2)], ssem.at[T_X])
    sent(xs_all.at[:, pl.ds(0, ROWS)], ssem.at[X_CORE])
    sent(xs_all.at[pl.ds(1, NC - 1), pl.ds(0, ROWS)], ssem.at[X_IN])
    yl_copy().wait_send()

    def wait_sent(k, carry):
        peer = (t + k) % 16
        place_copy(k, peer).wait_send()
        return carry

    lax.fori_loop(1, 16, wait_sent, 0)

    def wait_rows(k, carry):
        row_arrive(k)
        return carry

    lax.fori_loop(1, 16, wait_rows, 0)
    for part in range(2):
        out = lax.dot_general(
            pick_r[part], got[...], (((0,), (0,)), ((), ())), preferred_element_type=F32
        )
        out_ref[:, part * half : (part + 1) * half] = out.astype(BF16)

    def wait_rows_sent(k, carry):
        row_copy(k, (t + k) % 16).wait_send()
        return carry

    lax.fori_loop(1, 16, wait_rows_sent, 0)


def local(doc_rows, packed_slot, gate_weight, up_weight, down_weight):
    anywhere = pl.BlockSpec(memory_space=pl.ANY)
    vmem = pl.BlockSpec(memory_space=pltpu.VMEM)

    def buf(*shape, dtype=BF16):
        return pltpu.VMEM(shape, dtype)

    dma = pltpu.SemaphoreType.DMA
    return pl.pallas_call(
        kernel,
        out_shape=jax.ShapeDtypeStruct((ROWS, WIDTH), BF16),
        in_specs=[vmem, anywhere, anywhere, anywhere, anywhere],
        out_specs=vmem,
        scratch_shapes=[
            buf(2, TA + TB, WIDTH, TILE),
            buf(CA + CB, WIDTH),
            buf(NC, 128, WIDTH),
            buf(NC, 2, 2, 4, 16, CA),
            buf(NC, 2, 2, 4, 16, CB),
            buf(NC, 2, 2, 16, CA),
            buf(NC, 2, 2, 16, CA),
            buf(NC, 2, 2, 16, CA),
            buf(NC, 2, 2, 16, CA),
            buf(NC, 2, 16, CA),
            buf(NC, 2, 16, CA),
            buf(NC, 2, 4, 16, CB),
            buf(NC, 2, 4, 16, CB),
            buf(NC, 2, 16, CB),
            buf(NC, 2, 16, CB),
            buf(NC, 2, 16, CB),
            buf(NC, 2, 16, CB),
            buf(NC, 2, 4, 16, CA),
            buf(NC, 2, 4, 16, CB),
            buf(NC, 2, ROWS, WIDTH),
            buf(NC, ROWS, WIDTH),
            buf(NC, ROWS, WIDTH),
            buf(NC, ROWS, WIDTH),
            buf(2, ROWS, WIDTH, dtype=F32),
            buf(ROWS, WIDTH),
            buf(ROWS, WIDTH),
            buf(256, WIDTH // 2),
            buf(256, WIDTH // 2),
            buf(256, 128, dtype=jnp.int32),
            buf(256, 128, dtype=jnp.int32),
            buf(2, 256, ROWS),
            buf(2, 256, ROWS),
            dma((2, TA + TB)),
            dma,
            dma,
            dma((KINDS,)),
            dma((KINDS, NC)),
            dma,
            dma,
            dma((15,)),
            dma((15,)),
            dma((15,)),
            dma((15,)),
        ],
        compiler_params=pltpu.CompilerParams(
            collective_id=0, has_side_effects=True, vmem_limit_bytes=60 << 20
        ),
        cost_estimate=pl.CostEstimate(
            flops=2 * 1024 * 1024 * 5376, bytes_accessed=12 << 20, transcendentals=1024 * 1792 // 8
        ),
        name="layer",
    )(packed_slot.reshape(1, ROWS), doc_rows, gate_weight, up_weight, down_weight)


def solution(mesh):
    return jax.shard_map(
        local,
        mesh=mesh,
        in_specs=(
            P("tensor", "dp"),
            P("tensor"),
            P("dp", "tensor"),
            P("dp", "tensor"),
            P("tensor", "dp"),
        ),
        out_specs=P("tensor", "dp"),
        check_vma=False,
    )
```

```python
import jax
import jax.numpy as jnp
from jax import lax
from jax.experimental import pallas as pl
from jax.experimental.pallas import tpu as pltpu
from jax.sharding import PartitionSpec as P

MESH = pl.DeviceIdType.MESH
BF16 = jnp.bfloat16
F32 = jnp.float32

NC = 8
TILE = 256
TA = 4
TB = 3
CA = TA * TILE
CB = TB * TILE
HB2 = CB // 2
WIDTH = 1024
ROWS = 64

A_PT, A_PL, A_CB, A_Y = 0, 2, 4, 6
B_Y, B_PT, B_PL, B_CB = 7, 8, 10, 12
GA_Y, GA_Z, GA_F = 14, 15, 17
GB_Z, GB_F, GB_Y = 19, 21, 23
T_C, T_X, X_IN, X_CORE = 24, 25, 26, 27
KINDS = 28


ORDER = (
    0, 8, 17, 19, 1, 23, 9, 3, 18, 11, 22, 7, 27, 2, 136, 10, 21, 33, 31, 6,
    24, 35, 15, 51, 20, 26, 14, 4, 5, 12, 13, 34, 43, 28, 39, 38, 42, 67, 36, 30,
    59, 55, 50, 52, 46, 25, 58, 44, 47, 37, 75, 48, 29, 41, 66, 49, 83, 54, 68, 45,
    74, 60, 82, 62, 63, 91, 57, 99, 70, 71, 84, 61, 53, 64, 90, 76, 137, 98, 78, 32,
    86, 65, 107, 69, 79, 92, 100, 115, 77, 87, 106, 40, 73, 94, 102, 85, 95, 81, 93, 114,
    108, 103, 56, 116, 110, 89, 101, 118, 97, 80, 111, 72, 123, 122, 88, 119, 109, 105, 124, 117,
    126, 113, 128, 96, 104, 127, 112, 125,
)
DIRECT_SUM = (0,)
DIRECT_GATHER = (0,)


def kernel(
    slot_ref, doc_ref, gate_ref, up_ref, down_ref, out_ref,
    w1, wd, xs_all, pa, pb,
    pt_a, pl_a, cs_a, cr_a, ys_a, yr_a,
    yr_b, q_b, pt_b, pl_b, cs_b, cr_b,
    ha, hb, o2, o2r, xs, xr, acc, ysnd, yrcv,
    snd, got, pos_s, pos_g, pick_s, pick_r,
    wsem, dsem, lsem, ssem, rsem, tsend, trecv, psend, precv, gsend, grecv,
):
    dp = lax.axis_index("dp")
    t = lax.axis_index("tensor")
    z, yh = dp // 2, dp % 2
    x, yl, core = t // 4, (t // 2) % 2, t % 2
    zn, zb, z2 = (z + 1) % 4, (z + 3) % 4, (z + 2) % 4
    dev_z = ((zn * 2 + yh, t), (zb * 2 + yh, t))
    dev_z2 = (z2 * 2 + yh, t)
    dev_y = (z * 2 + 1 - yh, t)
    dev_core = (dp, t + 1 - 2 * core)
    dev_yl = (dp, t + 2 - 4 * yl)
    other = 1 - yh

    def dev_x(k):
        return (dp, ((x + k) % 4) * 4 + t % 4)

    def remote(src, dst, kind, c, device):
        return pltpu.make_async_remote_copy(
            src_ref=src, dst_ref=dst, send_sem=ssem.at[kind], recv_sem=rsem.at[kind, c],
            device_id=device, device_id_type=MESH,
        )

    def arrive(dst, kind, c):
        remote(dst, dst, kind, c, dev_y).wait_recv()

    own_x = xs_all.at[0, pl.ds(core * ROWS, ROWS)]
    doc_load = pltpu.make_async_copy(doc_ref, own_x, lsem)
    doc_load.start()

    def w_load(h, j):
        src = (gate_ref, up_ref)[h].at[:, pl.ds(pl.multiple_of(j * TILE, TILE), TILE)]
        return pltpu.make_async_copy(src, w1.at[h, j], wsem.at[h, j])

    def load_tile(j, carry):
        w_load(0, j).start()
        w_load(1, j).start()
        return carry

    lax.fori_loop(0, TA + TB, load_tile, 0)
    d_load = pltpu.make_async_copy(down_ref, wd, dsem)
    d_load.start()

    barrier = pltpu.get_barrier_semaphore()

    def greet(k, carry):
        pl.semaphore_signal(
            barrier, inc=1, device_id=(dp, (t + k) % 16), device_id_type=MESH
        )
        return carry

    lax.fori_loop(1, 16, greet, 0)
    for device in (dev_z[0], dev_z[1], dev_z2, dev_y):
        pl.semaphore_signal(barrier, inc=1, device_id=device, device_id_type=MESH)
    doc_load.wait()
    pl.semaphore_wait(barrier, 19)

    remote(own_x, own_x, X_CORE, 0, dev_core).start()
    remote(own_x, xs_all.at[1, pl.ds(core * ROWS, ROWS)], X_IN, 1, dev_yl).start()

    def x_slot(k, dy):
        return 2 * k + 1 - dy

    for k in (1, 3, 2):
        c = x_slot(k, 0)
        remote(own_x, xs_all.at[c, pl.ds(core * ROWS, ROWS)], X_IN, c, dev_x(4 - k)).start()

    def plan():
        slots = slot_ref[...]
        block = lax.shift_right_logical(slots, 6)
        place = slots & 63
        blocks = lax.broadcasted_iota(jnp.int32, (16, ROWS), 0)
        hot = jnp.where(blocks == block, 1.0, 0.0)
        before = jnp.where(
            lax.broadcasted_iota(jnp.int32, (ROWS, ROWS), 0)
            < lax.broadcasted_iota(jnp.int32, (ROWS, ROWS), 1),
            1.0,
            0.0,
        )
        count = jnp.dot(hot.astype(BF16), before.astype(BF16), preferred_element_type=F32)
        rank = jnp.sum(hot * count, axis=0, keepdims=True).astype(jnp.int32)
        return block, rank, place

    def send_places():
        block, rank, place = plan()
        q = lax.broadcasted_iota(jnp.int32, (256, ROWS), 0)
        home = block * 16 + rank
        pos = 0
        for half in range(2):
            pick = home + half * 8 == q
            pick_s[half] = jnp.where(pick, 1.0, 0.0).astype(BF16)
            pos += jnp.sum(jnp.where(pick, place + 1, 0), axis=1, keepdims=True)
        pos_s[...] = jnp.broadcast_to(pos - 1, (256, 128))

        def one(k, carry):
            place_copy(k, (t + k) % 16).start()
            return carry

        lax.fori_loop(1, 16, one, 0)
        pos_g[pl.ds(t * 16, 16)] = pos_s[pl.ds(t * 16, 16)]

    def take_places():
        def one(k, carry):
            place_arrive(k)
            return carry

        lax.fori_loop(1, 16, one, 0)
        q = lax.broadcasted_iota(jnp.int32, (256, ROWS), 0)
        here = pos_g[:, 0:ROWS] == lax.broadcasted_iota(jnp.int32, (256, ROWS), 1)
        for half in range(2):
            pick_r[half] = jnp.where(here & ((q // 8) % 2 == half), 1.0, 0.0).astype(BF16)

    def place_copy(k, peer):
        return pltpu.make_async_remote_copy(
            src_ref=pos_s.at[pl.ds(peer * 16, 16)], dst_ref=pos_g.at[pl.ds(t * 16, 16)],
            send_sem=psend.at[k - 1], recv_sem=precv.at[k - 1], device_id=(dp, peer), device_id_type=MESH,
        )

    def place_arrive(k):
        rows = pos_g.at[pl.ds(((t + 16 - k) % 16) * 16, 16)]
        pltpu.make_async_remote_copy(
            src_ref=rows, dst_ref=rows, send_sem=psend.at[k - 1], recv_sem=precv.at[k - 1],
            device_id=dev_y, device_id_type=MESH,
        ).wait_recv()

    def row_copy(k, peer):
        return pltpu.make_async_remote_copy(
            src_ref=snd.at[pl.ds(peer * 16, 16)], dst_ref=got.at[pl.ds(t * 16, 16)],
            send_sem=gsend.at[k - 1], recv_sem=grecv.at[k - 1], device_id=(dp, peer), device_id_type=MESH,
        )

    def row_arrive(k):
        rows = got.at[pl.ds(((t + 16 - k) % 16) * 16, 16)]
        pltpu.make_async_remote_copy(
            src_ref=rows, dst_ref=rows, send_sem=gsend.at[k - 1], recv_sem=grecv.at[k - 1],
            device_id=dev_y, device_id_type=MESH,
        ).wait_recv()

    first = set()

    def once(name):
        new = name not in first
        first.add(name)
        return new

    def gate_up(c, dst, base, count):
        fresh = once(base)

        def tile(j, carry):
            for h in range(2):
                if fresh:
                    w_load(h, base + j).wait()
                r = jnp.dot(xs_all[c], w1[h, base + j], preferred_element_type=F32)
                cols = pl.ds(pl.multiple_of(j * TILE, TILE), TILE)
                dst[c, h, :, :, :, cols] = r.astype(BF16).reshape(2, 4, 16, TILE)
            return carry

        lax.fori_loop(0, count, tile, 0)

    def step_0a(c):
        arrive(xs_all.at[c, pl.ds((1 - core) * ROWS, ROWS)], X_CORE, c)
        gate_up(c, pa, 0, TA)
        for d in range(2):
            via = dev_z2 if c in DIRECT_SUM else dev_z[d]
            remote(pa.at[c, d, :, z2], pt_a.at[c, d], A_PT + d, c, via).start()
        for d in range(2):
            near = (zn, zb)[d]
            remote(pa.at[c, 1 - d, :, near], pl_a.at[c, d], A_PL + d, c, dev_z[d]).start()
            if c in DIRECT_SUM:
                remote(pa.at[c, d, :, near], cr_a.at[c, d], A_CB + d, c, dev_z[d]).start()

    def step_0b(c):
        gate_up(c, pb, TA, TB)
        remote(pb.at[c, :, other], yr_b.at[c], B_Y, c, dev_y).start()

    def next_rows(c):
        rows = xs_all.at[c, pl.ds(core * ROWS, ROWS)]
        arrive(rows, X_IN, c)
        remote(rows, rows, X_CORE, c, dev_core).start()
        if c == 1:
            for k in (1, 3, 2):
                far = x_slot(k, 1)
                remote(rows, xs_all.at[far, pl.ds(core * ROWS, ROWS)], X_IN, far, dev_x(4 - k)).start()

    def step_1a(c):
        for d in range(2):
            near = (zn, zb)[d]
            arrive(pt_a.at[c, d], A_PT + d, c)
            if c in DIRECT_SUM:
                continue
            cs_a[c, d] = (pa[c, d, :, near].astype(F32) + pt_a[c, d].astype(F32)).astype(BF16)
            remote(cs_a.at[c, d], cr_a.at[c, d], A_CB + d, c, dev_z[d]).start()

    def step_1b(c):
        arrive(yr_b.at[c], B_Y, c)
        q_b[c] = (pb[c, :, yh].astype(F32) + yr_b[c].astype(F32)).astype(BF16)
        for d in range(2):
            remote(q_b.at[c, d, z2], pt_b.at[c, d], B_PT + d, c, dev_z[d]).start()
        for d in range(2):
            near = (zn, zb)[d]
            remote(q_b.at[c, 1 - d, near], pl_b.at[c, d], B_PL + d, c, dev_z[d]).start()

    def z_sum_a(c, h, y):
        total = (
            pa[c, h, y, z].astype(F32)
            + cr_a[c, h, y].astype(F32)
            + pl_a[c, 1 - h, y].astype(F32)
        )
        return total + pt_a[c, h, y].astype(F32) if c in DIRECT_SUM else total

    def step_2b(c):
        for d in range(2):
            near = (zn, zb)[d]
            arrive(pt_b.at[c, d], B_PT + d, c)
            cs_b[c, d] = (q_b[c, d, near].astype(F32) + pt_b[c, d].astype(F32)).astype(BF16)
            remote(cs_b.at[c, d], cr_b.at[c, d], B_CB + d, c, dev_z[d]).start()

    def step_2a(c):
        for d in range(2):
            arrive(pl_a.at[c, d], A_PL + d, c)
            arrive(cr_a.at[c, d], A_CB + d, c)
        for h in range(2):
            ys_a[c, h] = z_sum_a(c, h, other).astype(BF16)
        remote(ys_a.at[c], yr_a.at[c], A_Y, c, dev_y).start()

    def gated(g, u):
        return (g / (1.0 + jnp.exp(-g)) * u).astype(BF16)

    def step_3b(c):
        for d in range(2):
            arrive(pl_b.at[c, d], B_PL + d, c)
            arrive(cr_b.at[c, d], B_CB + d, c)
        g, u = (
            q_b[c, h, z].astype(F32) + cr_b[c, h].astype(F32) + pl_b[c, 1 - h].astype(F32)
            for h in range(2)
        )
        hb[c, yh, z] = gated(g, u)
        for d in range(2):
            remote(hb.at[c, yh, z], hb.at[c, yh, z], GB_Z + d, c, dev_z[d]).start()
        if c in DIRECT_GATHER:
            for d in range(2):
                part = hb.at[c, yh, z, :, pl.ds(d * HB2, HB2)]
                remote(part, part, GB_F + d, c, dev_z2).start()

    def step_3a(c):
        arrive(yr_a.at[c], A_Y, c)
        g, u = (z_sum_a(c, h, yh) + yr_a[c, h].astype(F32) for h in range(2))
        ha[c, yh, z] = gated(g, u)
        remote(ha.at[c, yh, z], ha.at[c, yh, z], GA_Y, c, dev_y).start()

    def step_4b(c):
        for d in range(2):
            back = (zb, zn)[d]
            arrive(hb.at[c, yh, back], GB_Z + d, c)
            if c in DIRECT_GATHER:
                continue
            part = hb.at[c, yh, back, :, pl.ds(d * HB2, HB2)]
            remote(part, part, GB_F + d, c, dev_z[d]).start()

    def step_4a(c):
        arrive(ha.at[c, other, z], GA_Y, c)
        for d in range(2):
            remote(ha.at[c, :, z], ha.at[c, :, z], GA_Z + d, c, dev_z[d]).start()
        if c in DIRECT_GATHER:
            for d in range(2):
                remote(ha.at[c, d, z], ha.at[c, d, z], GA_F + d, c, dev_z2).start()

    def step_5b(c):
        for d in range(2):
            arrive(hb.at[c, yh, z2, :, pl.ds(d * HB2, HB2)], GB_F + d, c)
        remote(hb.at[c, yh], hb.at[c, yh], GB_Y, c, dev_y).start()

    def step_5a(c):
        for d in range(2):
            back = (zb, zn)[d]
            arrive(ha.at[c, :, back], GA_Z + d, c)
            if c in DIRECT_GATHER:
                continue
            part = ha.at[c, d, back]
            remote(part, part, GA_F + d, c, dev_z[d]).start()

    def step_6(c):
        for d in range(2):
            arrive(ha.at[c, d, z2], GA_F + d, c)
        arrive(hb.at[c, other], GB_Y, c)
        if once("down"):
            d_load.wait()

        def tile(n, carry):
            cols = pl.ds(pl.multiple_of(n * TILE, TILE), TILE)
            r = jnp.dot(ha[c].reshape(128, CA), wd[0:CA, cols], preferred_element_type=F32)
            r += jnp.dot(hb[c].reshape(128, CB), wd[CA : CA + CB, cols], preferred_element_type=F32)
            o2[c, :, :, cols] = r.astype(BF16).reshape(2, ROWS, TILE)
            return carry

        lax.fori_loop(0, WIDTH // TILE, tile, 0)
        remote(o2.at[c, 1 - core], o2r.at[c], T_C, c, dev_core).start()

    def add(dy, value):
        acc[dy] = value if once(("acc", dy)) else acc[dy] + value

    def step_7(c):
        arrive(o2r.at[c], T_C, c)
        total = o2[c, core].astype(F32) + o2r[c].astype(F32)
        if c < 2:
            add(c, total)
        else:
            xs[c] = total.astype(BF16)
            remote(xs.at[c], xr.at[c], T_X, c, dev_x(c // 2)).start()

    def step_8(c):
        arrive(xr.at[c], T_X, c)
        add((c + 1) % 2, xr[c].astype(F32))

    def yl_copy():
        return pltpu.make_async_remote_copy(
            src_ref=ysnd, dst_ref=yrcv, send_sem=tsend, recv_sem=trecv, device_id=dev_yl, device_id_type=MESH
        )

    def step_y(c):
        ysnd[...] = acc[1].astype(BF16)
        yl_copy().start()

    def step_p(c):
        send_places() if c == 0 else take_places()

    steps = (
        step_0a, step_0b, next_rows, step_1a, step_1b, step_2b, step_2a, step_3b, step_3a,
        step_4b, step_4a, step_5b, step_5a, step_6, step_7, step_8, step_y, step_p,
    )
    for entry in ORDER:
        steps[entry // 8](entry % 8)

    yl_copy().wait_recv()
    rows = (
        xs_all[0, pl.ds(core * ROWS, ROWS)].astype(F32)
        + acc[0]
        + yrcv[...].astype(F32)
    ).astype(BF16)
    half = WIDTH // 2
    packed = jnp.dot(pick_s[0], rows[:, :half], preferred_element_type=F32)
    packed += jnp.dot(pick_s[1], rows[:, half:], preferred_element_type=F32)
    snd[...] = packed.astype(BF16)

    def start_rows(i, carry):
        k = (i + 6) % 15 + 1
        row_copy(k, (t + k) % 16).start()
        return carry

    lax.fori_loop(1, 16, start_rows, 0)
    got[pl.ds(t * 16, 16)] = snd[pl.ds(t * 16, 16)]

    def sent(ref, sem):
        pltpu.make_async_copy(ref, ref, sem).wait()

    for d in range(2):
        sent(pt_a.at[:, d], ssem.at[A_PT + d])
        sent(pl_a.at[:, d], ssem.at[A_PL + d])
        sent(cr_a.at[:, d], ssem.at[A_CB + d])
        sent(pt_b.at[:, d], ssem.at[B_PT + d])
        sent(pl_b.at[:, d], ssem.at[B_PL + d])
        sent(cr_b.at[:, d], ssem.at[B_CB + d])
        sent(ha.at[:, :, 0], ssem.at[GA_Z + d])
        sent(ha.at[:, 0, 0], ssem.at[GA_F + d])
        sent(hb.at[:, 0, 0], ssem.at[GB_Z + d])
        sent(hb.at[:, 0, 0, :, pl.ds(0, HB2)], ssem.at[GB_F + d])
    sent(yr_a, ssem.at[A_Y])
    sent(yr_b, ssem.at[B_Y])
    sent(ha.at[:, 0, 0], ssem.at[GA_Y])
    sent(hb.at[:, 0], ssem.at[GB_Y])
    sent(o2r, ssem.at[T_C])
    sent(xr.at[pl.ds(2, NC - 2)], ssem.at[T_X])
    sent(xs_all.at[:, pl.ds(0, ROWS)], ssem.at[X_CORE])
    sent(xs_all.at[pl.ds(1, NC - 1), pl.ds(0, ROWS)], ssem.at[X_IN])
    yl_copy().wait_send()

    def wait_sent(k, carry):
        peer = (t + k) % 16
        place_copy(k, peer).wait_send()
        return carry

    lax.fori_loop(1, 16, wait_sent, 0)

    def wait_rows(k, carry):
        row_arrive(k)
        return carry

    lax.fori_loop(1, 16, wait_rows, 0)
    for part in range(2):
        out = lax.dot_general(
            pick_r[part], got[...], (((0,), (0,)), ((), ())), preferred_element_type=F32
        )
        out_ref[:, part * half : (part + 1) * half] = out.astype(BF16)

    def wait_rows_sent(k, carry):
        row_copy(k, (t + k) % 16).wait_send()
        return carry

    lax.fori_loop(1, 16, wait_rows_sent, 0)


def local(doc_rows, packed_slot, gate_weight, up_weight, down_weight):
    anywhere = pl.BlockSpec(memory_space=pl.ANY)
    vmem = pl.BlockSpec(memory_space=pltpu.VMEM)

    def buf(*shape, dtype=BF16):
        return pltpu.VMEM(shape, dtype)

    dma = pltpu.SemaphoreType.DMA
    return pl.pallas_call(
        kernel,
        out_shape=jax.ShapeDtypeStruct((ROWS, WIDTH), BF16),
        in_specs=[vmem, anywhere, anywhere, anywhere, anywhere],
        out_specs=vmem,
        scratch_shapes=[
            buf(2, TA + TB, WIDTH, TILE),
            buf(CA + CB, WIDTH),
            buf(NC, 128, WIDTH),
            buf(NC, 2, 2, 4, 16, CA),
            buf(NC, 2, 2, 4, 16, CB),
            buf(NC, 2, 2, 16, CA),
            buf(NC, 2, 2, 16, CA),
            buf(NC, 2, 2, 16, CA),
            buf(NC, 2, 2, 16, CA),
            buf(NC, 2, 16, CA),
            buf(NC, 2, 16, CA),
            buf(NC, 2, 4, 16, CB),
            buf(NC, 2, 4, 16, CB),
            buf(NC, 2, 16, CB),
            buf(NC, 2, 16, CB),
            buf(NC, 2, 16, CB),
            buf(NC, 2, 16, CB),
            buf(NC, 2, 4, 16, CA),
            buf(NC, 2, 4, 16, CB),
            buf(NC, 2, ROWS, WIDTH),
            buf(NC, ROWS, WIDTH),
            buf(NC, ROWS, WIDTH),
            buf(NC, ROWS, WIDTH),
            buf(2, ROWS, WIDTH, dtype=F32),
            buf(ROWS, WIDTH),
            buf(ROWS, WIDTH),
            buf(256, WIDTH // 2),
            buf(256, WIDTH // 2),
            buf(256, 128, dtype=jnp.int32),
            buf(256, 128, dtype=jnp.int32),
            buf(2, 256, ROWS),
            buf(2, 256, ROWS),
            dma((2, TA + TB)),
            dma,
            dma,
            dma((KINDS,)),
            dma((KINDS, NC)),
            dma,
            dma,
            dma((15,)),
            dma((15,)),
            dma((15,)),
            dma((15,)),
        ],
        compiler_params=pltpu.CompilerParams(
            collective_id=0, has_side_effects=True, vmem_limit_bytes=60 << 20
        ),
        cost_estimate=pl.CostEstimate(
            flops=2 * 1024 * 1024 * 5376, bytes_accessed=12 << 20, transcendentals=1024 * 1792 // 8
        ),
        name="layer",
    )(packed_slot.reshape(1, ROWS), doc_rows, gate_weight, up_weight, down_weight)


def solution(mesh):
    return jax.shard_map(
        local,
        mesh=mesh,
        in_specs=(
            P("tensor", "dp"),
            P("tensor"),
            P("dp", "tensor"),
            P("dp", "tensor"),
            P("tensor", "dp"),
        ),
        out_specs=P("tensor", "dp"),
        check_vma=False,
    )
```

```python
import jax
import jax.numpy as jnp
from jax import lax
from jax.experimental import pallas as pl
from jax.experimental.pallas import tpu as pltpu
from jax.sharding import PartitionSpec as P

MESH = pl.DeviceIdType.MESH
BF16 = jnp.bfloat16
F32 = jnp.float32

NC = 8
TILE = 256
TA = 4
TB = 3
CA = TA * TILE
CB = TB * TILE
HB2 = CB // 2
WIDTH = 1024
ROWS = 64

A_PT, A_PL, A_CB, A_Y, B_Y, B_PT, B_PL, B_CB = (0, 0), (1, 1), (2, 1), (3, 2), (4, 3), (5, 4), (6, 5), (7, 5)
GA_Y, GA_F, GB_F, GB_Y = (8, 6), (9, 7), (10, 8), (11, 9)
T_C, T_X, X_IN, X_CORE = (12, 10), (13, 11), (14, 12), (15, 13)
GA_Z = ((16, 14), (16, 15))
GB_Z = ((17, 16), (17, 17))
KINDS = 18


ORDER = (
    0, 8, 136, 17, 19, 1, 3, 11, 24, 23, 7, 15, 18, 27, 20, 4, 12, 2, 48, 51,
    35, 10, 31, 22, 36, 28, 21, 6, 5, 14, 137, 13, 43, 44, 52, 67, 34, 26, 38, 9,
    60, 59, 42, 39, 29, 30, 46, 50, 68, 55, 47, 25, 58, 32, 53, 62, 76, 54, 37, 84,
    66, 75, 33, 83, 71, 74, 92, 70, 63, 45, 100, 78, 49, 82, 91, 41, 69, 79, 99, 90,
    61, 86, 108, 98, 57, 65, 87, 40, 94, 95, 107, 77, 116, 102, 85, 106, 103, 115, 64, 93,
    73, 81, 56, 114, 110, 101, 89, 111, 97, 118, 124, 80, 109, 72, 119, 88, 105, 122, 96, 117,
    126, 113, 128, 104, 112, 123, 125, 127,
)
DIRECT_SUM = (0,)
DIRECT_GATHER = (0,)


def kernel(
    slot_ref, doc_ref, gate_ref, up_ref, down_ref, out_ref,
    w1, wd, xs_all, pa, pb,
    pt_a, pc_a, cs_a, ys_a, yr_a,
    yr_b, q_b, pt_b, pc_b, cs_b,
    ha, hb, o2, o2r, xs, xr, acc, ysnd, yrcv,
    snd, got, pos_s, pos_g, pick_s, pick_r,
    wsem, dsem, lsem, ssem, rsem, tsend, trecv, psend, precv, gsend, grecv,
):
    dp = lax.axis_index("dp")
    t = lax.axis_index("tensor")
    z, yh = dp // 2, dp % 2
    x, yl, core = t // 4, (t // 2) % 2, t % 2
    zn, zb, z2 = (z + 1) % 4, (z + 3) % 4, (z + 2) % 4
    dev_z = ((zn * 2 + yh, t), (zb * 2 + yh, t))
    dev_z2 = (z2 * 2 + yh, t)
    dev_y = (z * 2 + 1 - yh, t)
    dev_core = (dp, t + 1 - 2 * core)
    dev_yl = (dp, t + 2 - 4 * yl)
    other = 1 - yh

    def dev_x(k):
        return (dp, ((x + k) % 4) * 4 + t % 4)

    def remote(src, dst, kind, c, device):
        return pltpu.make_async_remote_copy(
            src_ref=src, dst_ref=dst, send_sem=ssem.at[kind[0]], recv_sem=rsem.at[kind[1], c],
            device_id=device, device_id_type=MESH,
        )

    def arrive(dst, kind, c):
        remote(dst, dst, kind, c, dev_y).wait_recv()

    own_x = xs_all.at[0, pl.ds(core * ROWS, ROWS)]
    doc_load = pltpu.make_async_copy(doc_ref, own_x, lsem)
    doc_load.start()

    def w_load(h, j):
        src = (gate_ref, up_ref)[h].at[:, pl.ds(pl.multiple_of(j * TILE, TILE), TILE)]
        return pltpu.make_async_copy(src, w1.at[h, j], wsem.at[j])

    def load_tile(j, carry):
        w_load(0, j).start()
        w_load(1, j).start()
        return carry

    lax.fori_loop(0, TA + TB, load_tile, 0)
    d_load = pltpu.make_async_copy(down_ref, wd, dsem)
    d_load.start()

    barrier = pltpu.get_barrier_semaphore()

    def greet(k, carry):
        pl.semaphore_signal(
            barrier, inc=1, device_id=(dp, (t + k) % 16), device_id_type=MESH
        )
        return carry

    lax.fori_loop(1, 16, greet, 0)
    for device in (dev_z[0], dev_z[1], dev_z2, dev_y):
        pl.semaphore_signal(barrier, inc=1, device_id=device, device_id_type=MESH)
    doc_load.wait()
    pl.semaphore_wait(barrier, 19)

    remote(own_x, own_x, X_CORE, 0, dev_core).start()
    remote(own_x, xs_all.at[1, pl.ds(core * ROWS, ROWS)], X_IN, 1, dev_yl).start()

    def x_slot(k, dy):
        return 2 * k + 1 - dy

    for k in (1, 3, 2):
        c = x_slot(k, 0)
        remote(own_x, xs_all.at[c, pl.ds(core * ROWS, ROWS)], X_IN, c, dev_x(4 - k)).start()

    def plan():
        slots = slot_ref[...]
        block = lax.shift_right_logical(slots, 6)
        place = slots & 63
        blocks = lax.broadcasted_iota(jnp.int32, (16, ROWS), 0)
        hot = jnp.where(blocks == block, 1.0, 0.0)
        before = jnp.where(
            lax.broadcasted_iota(jnp.int32, (ROWS, ROWS), 0)
            < lax.broadcasted_iota(jnp.int32, (ROWS, ROWS), 1),
            1.0,
            0.0,
        )
        count = jnp.dot(hot.astype(BF16), before.astype(BF16), preferred_element_type=F32)
        rank = jnp.sum(hot * count, axis=0, keepdims=True).astype(jnp.int32)
        return block, rank, place

    def send_places():
        block, rank, place = plan()
        q = lax.broadcasted_iota(jnp.int32, (256, ROWS), 0)
        home = block * 16 + rank
        pos = 0
        for half in range(2):
            pick = home + half * 8 == q
            pick_s[half] = jnp.where(pick, 1.0, 0.0).astype(BF16)
            pos += jnp.sum(jnp.where(pick, place + 1, 0), axis=1, keepdims=True)
        pos_s[...] = jnp.broadcast_to(pos - 1, (256, 128))

        def one(k, carry):
            place_copy(k, (t + k) % 16).start()
            return carry

        lax.fori_loop(1, 16, one, 0)
        pos_g[pl.ds(t * 16, 16)] = pos_s[pl.ds(t * 16, 16)]

    def take_places():
        all_peers(pos_g, precv)
        q = lax.broadcasted_iota(jnp.int32, (256, ROWS), 0)
        here = pos_g[:, 0:ROWS] == lax.broadcasted_iota(jnp.int32, (256, ROWS), 1)
        for half in range(2):
            pick_r[half] = jnp.where(here & ((q // 8) % 2 == half), 1.0, 0.0).astype(BF16)

    def place_copy(k, peer):
        return pltpu.make_async_remote_copy(
            src_ref=pos_s.at[pl.ds(peer * 16, 16)], dst_ref=pos_g.at[pl.ds(t * 16, 16)],
            send_sem=psend, recv_sem=precv, device_id=(dp, peer), device_id_type=MESH,
        )

    def row_copy(k, peer):
        return pltpu.make_async_remote_copy(
            src_ref=snd.at[pl.ds(peer * 16, 16)], dst_ref=got.at[pl.ds(t * 16, 16)],
            send_sem=gsend, recv_sem=grecv, device_id=(dp, peer), device_id_type=MESH,
        )

    def all_peers(ref, sem):
        rows = ref.at[pl.ds(0, 240)]
        pltpu.make_async_copy(rows, rows, sem).wait()

    first = set()

    def once(name):
        new = name not in first
        first.add(name)
        return new

    def gate_up(c, dst, base, count):
        fresh = once(base)

        def tile(j, carry):
            if fresh:
                pair = w1.at[:, base + j]
                pltpu.make_async_copy(pair, pair, wsem.at[base + j]).wait()
            for h in range(2):
                r = jnp.dot(xs_all[c], w1[h, base + j], preferred_element_type=F32)
                cols = pl.ds(pl.multiple_of(j * TILE, TILE), TILE)
                dst[c, h, :, :, :, cols] = r.astype(BF16).reshape(2, 4, 16, TILE)
            return carry

        lax.fori_loop(0, count, tile, 0)

    def step_0a(c):
        arrive(xs_all.at[c, pl.ds((1 - core) * ROWS, ROWS)], X_CORE, c)
        gate_up(c, pa, 0, TA)
        for d in range(2):
            via = dev_z2 if c in DIRECT_SUM else dev_z[d]
            remote(pa.at[c, d, :, z2], pt_a.at[c, d], A_PT, c, via).start()
        for d in range(2):
            near = (zn, zb)[d]
            remote(pa.at[c, 1 - d, :, near], pc_a.at[c, 0, d], A_PL, c, dev_z[d]).start()
            if c in DIRECT_SUM:
                remote(pa.at[c, d, :, near], pc_a.at[c, 1, d], A_CB, c, dev_z[d]).start()

    def step_0b(c):
        gate_up(c, pb, TA, TB)
        remote(pb.at[c, :, other], yr_b.at[c], B_Y, c, dev_y).start()

    def next_rows(c):
        rows = xs_all.at[c, pl.ds(core * ROWS, ROWS)]
        arrive(rows, X_IN, c)
        remote(rows, rows, X_CORE, c, dev_core).start()
        if c == 1:
            for k in (1, 3, 2):
                far = x_slot(k, 1)
                remote(rows, xs_all.at[far, pl.ds(core * ROWS, ROWS)], X_IN, far, dev_x(4 - k)).start()

    def step_1a(c):
        arrive(pt_a.at[c], A_PT, c)
        if c in DIRECT_SUM:
            return
        for d in range(2):
            near = (zn, zb)[d]
            cs_a[c, d] = (pa[c, d, :, near].astype(F32) + pt_a[c, d].astype(F32)).astype(BF16)
            remote(cs_a.at[c, d], pc_a.at[c, 1, d], A_CB, c, dev_z[d]).start()

    def step_1b(c):
        arrive(yr_b.at[c], B_Y, c)
        q_b[c] = (pb[c, :, yh].astype(F32) + yr_b[c].astype(F32)).astype(BF16)
        for d in range(2):
            remote(q_b.at[c, d, z2], pt_b.at[c, d], B_PT, c, dev_z[d]).start()
        for d in range(2):
            near = (zn, zb)[d]
            remote(q_b.at[c, 1 - d, near], pc_b.at[c, 0, d], B_PL, c, dev_z[d]).start()

    def z_sum_a(c, h, y):
        total = (
            pa[c, h, y, z].astype(F32)
            + pc_a[c, 1, h, y].astype(F32)
            + pc_a[c, 0, 1 - h, y].astype(F32)
        )
        return total + pt_a[c, h, y].astype(F32) if c in DIRECT_SUM else total

    def step_2b(c):
        arrive(pt_b.at[c], B_PT, c)
        for d in range(2):
            near = (zn, zb)[d]
            cs_b[c, d] = (q_b[c, d, near].astype(F32) + pt_b[c, d].astype(F32)).astype(BF16)
            remote(cs_b.at[c, d], pc_b.at[c, 1, d], B_CB, c, dev_z[d]).start()

    def step_2a(c):
        arrive(pc_a.at[c], A_PL, c)
        for h in range(2):
            ys_a[c, h] = z_sum_a(c, h, other).astype(BF16)
        remote(ys_a.at[c], yr_a.at[c], A_Y, c, dev_y).start()

    def gated(g, u):
        return (g / (1.0 + jnp.exp(-g)) * u).astype(BF16)

    def step_3b(c):
        arrive(pc_b.at[c], B_PL, c)
        g, u = (
            q_b[c, h, z].astype(F32) + pc_b[c, 1, h].astype(F32) + pc_b[c, 0, 1 - h].astype(F32)
            for h in range(2)
        )
        hb[c, yh, z] = gated(g, u)
        for d in range(2):
            remote(hb.at[c, yh, z], hb.at[c, yh, z], GB_Z[d], c, dev_z[d]).start()
        if c in DIRECT_GATHER:
            for d in range(2):
                part = hb.at[c, yh, z, :, pl.ds(d * HB2, HB2)]
                remote(part, part, GB_F, c, dev_z2).start()

    def step_3a(c):
        arrive(yr_a.at[c], A_Y, c)
        g, u = (z_sum_a(c, h, yh) + yr_a[c, h].astype(F32) for h in range(2))
        ha[c, yh, z] = gated(g, u)
        remote(ha.at[c, yh, z], ha.at[c, yh, z], GA_Y, c, dev_y).start()

    def step_4b(c):
        for d in range(2):
            back = (zb, zn)[d]
            arrive(hb.at[c, yh, back], GB_Z[d], c)
            if c in DIRECT_GATHER:
                continue
            part = hb.at[c, yh, back, :, pl.ds(d * HB2, HB2)]
            remote(part, part, GB_F, c, dev_z[d]).start()

    def step_4a(c):
        arrive(ha.at[c, other, z], GA_Y, c)
        for d in range(2):
            remote(ha.at[c, :, z], ha.at[c, :, z], GA_Z[d], c, dev_z[d]).start()
        if c in DIRECT_GATHER:
            for d in range(2):
                remote(ha.at[c, d, z], ha.at[c, d, z], GA_F, c, dev_z2).start()

    def step_5b(c):
        arrive(hb.at[c, yh, z2], GB_F, c)
        remote(hb.at[c, yh], hb.at[c, yh], GB_Y, c, dev_y).start()

    def step_5a(c):
        for d in range(2):
            back = (zb, zn)[d]
            arrive(ha.at[c, :, back], GA_Z[d], c)
            if c in DIRECT_GATHER:
                continue
            part = ha.at[c, d, back]
            remote(part, part, GA_F, c, dev_z[d]).start()

    def step_6(c):
        arrive(ha.at[c, :, z2], GA_F, c)
        arrive(hb.at[c, other], GB_Y, c)
        if once("down"):
            d_load.wait()

        def tile(n, carry):
            cols = pl.ds(pl.multiple_of(n * TILE, TILE), TILE)
            r = jnp.dot(ha[c].reshape(128, CA), wd[0:CA, cols], preferred_element_type=F32)
            r += jnp.dot(hb[c].reshape(128, CB), wd[CA : CA + CB, cols], preferred_element_type=F32)
            o2[c, :, :, cols] = r.astype(BF16).reshape(2, ROWS, TILE)
            return carry

        lax.fori_loop(0, WIDTH // TILE, tile, 0)
        remote(o2.at[c, 1 - core], o2r.at[c], T_C, c, dev_core).start()

    def add(dy, value):
        acc[dy] = value if once(("acc", dy)) else acc[dy] + value

    def step_7(c):
        arrive(o2r.at[c], T_C, c)
        total = o2[c, core].astype(F32) + o2r[c].astype(F32)
        if c < 2:
            add(c, total)
        else:
            xs[c] = total.astype(BF16)
            remote(xs.at[c], xr.at[c], T_X, c, dev_x(c // 2)).start()

    def step_8(c):
        arrive(xr.at[c], T_X, c)
        add((c + 1) % 2, xr[c].astype(F32))

    def yl_copy():
        return pltpu.make_async_remote_copy(
            src_ref=ysnd, dst_ref=yrcv, send_sem=tsend, recv_sem=trecv, device_id=dev_yl, device_id_type=MESH
        )

    def step_y(c):
        ysnd[...] = acc[1].astype(BF16)
        yl_copy().start()

    def step_p(c):
        send_places() if c == 0 else take_places()

    steps = (
        step_0a, step_0b, next_rows, step_1a, step_1b, step_2b, step_2a, step_3b, step_3a,
        step_4b, step_4a, step_5b, step_5a, step_6, step_7, step_8, step_y, step_p,
    )
    for entry in ORDER:
        steps[entry // 8](entry % 8)

    yl_copy().wait_recv()
    rows = (
        xs_all[0, pl.ds(core * ROWS, ROWS)].astype(F32)
        + acc[0]
        + yrcv[...].astype(F32)
    ).astype(BF16)
    half = WIDTH // 2
    packed = jnp.dot(pick_s[0], rows[:, :half], preferred_element_type=F32)
    packed += jnp.dot(pick_s[1], rows[:, half:], preferred_element_type=F32)
    snd[...] = packed.astype(BF16)

    def start_rows(i, carry):
        k = (i + 6) % 15 + 1
        row_copy(k, (t + k) % 16).start()
        return carry

    lax.fori_loop(1, 16, start_rows, 0)
    got[pl.ds(t * 16, 16)] = snd[pl.ds(t * 16, 16)]

    def sent(ref, sem):
        pltpu.make_async_copy(ref, ref, sem).wait()

    sent(pt_a, ssem.at[A_PT[0]])
    sent(pc_a.at[:, 0], ssem.at[A_PL[0]])
    sent(pc_a.at[:, 1], ssem.at[A_CB[0]])
    sent(pt_b, ssem.at[B_PT[0]])
    sent(pc_b.at[:, 0], ssem.at[B_PL[0]])
    sent(pc_b.at[:, 1], ssem.at[B_CB[0]])
    sent(ha.at[:, :, pl.ds(0, 2)], ssem.at[GA_Z[0][0]])
    sent(ha.at[:, :, 0], ssem.at[GA_F[0]])
    sent(hb.at[:, 0, pl.ds(0, 2)], ssem.at[GB_Z[0][0]])
    sent(hb.at[:, 0, 0], ssem.at[GB_F[0]])
    sent(yr_a, ssem.at[A_Y[0]])
    sent(yr_b, ssem.at[B_Y[0]])
    sent(ha.at[:, 0, 0], ssem.at[GA_Y[0]])
    sent(hb.at[:, 0], ssem.at[GB_Y[0]])
    sent(o2r, ssem.at[T_C[0]])
    sent(xr.at[pl.ds(2, NC - 2)], ssem.at[T_X[0]])
    sent(xs_all.at[:, pl.ds(0, ROWS)], ssem.at[X_CORE[0]])
    sent(xs_all.at[pl.ds(1, NC - 1), pl.ds(0, ROWS)], ssem.at[X_IN[0]])
    yl_copy().wait_send()

    all_peers(pos_s, psend)
    all_peers(got, grecv)
    for part in range(2):
        out = lax.dot_general(
            pick_r[part], got[...], (((0,), (0,)), ((), ())), preferred_element_type=F32
        )
        out_ref[:, part * half : (part + 1) * half] = out.astype(BF16)

    all_peers(snd, gsend)


def local(doc_rows, packed_slot, gate_weight, up_weight, down_weight):
    anywhere = pl.BlockSpec(memory_space=pl.ANY)
    vmem = pl.BlockSpec(memory_space=pltpu.VMEM)

    def buf(*shape, dtype=BF16):
        return pltpu.VMEM(shape, dtype)

    dma = pltpu.SemaphoreType.DMA
    return pl.pallas_call(
        kernel,
        out_shape=jax.ShapeDtypeStruct((ROWS, WIDTH), BF16),
        in_specs=[vmem, anywhere, anywhere, anywhere, anywhere],
        out_specs=vmem,
        scratch_shapes=[
            buf(2, TA + TB, WIDTH, TILE),
            buf(CA + CB, WIDTH),
            buf(NC, 128, WIDTH),
            buf(NC, 2, 2, 4, 16, CA),
            buf(NC, 2, 2, 4, 16, CB),
            buf(NC, 2, 2, 16, CA),
            buf(NC, 2, 2, 2, 16, CA),
            buf(NC, 2, 2, 16, CA),
            buf(NC, 2, 16, CA),
            buf(NC, 2, 16, CA),
            buf(NC, 2, 4, 16, CB),
            buf(NC, 2, 4, 16, CB),
            buf(NC, 2, 16, CB),
            buf(NC, 2, 2, 16, CB),
            buf(NC, 2, 16, CB),
            buf(NC, 2, 4, 16, CA),
            buf(NC, 2, 4, 16, CB),
            buf(NC, 2, ROWS, WIDTH),
            buf(NC, ROWS, WIDTH),
            buf(NC, ROWS, WIDTH),
            buf(NC, ROWS, WIDTH),
            buf(2, ROWS, WIDTH, dtype=F32),
            buf(ROWS, WIDTH),
            buf(ROWS, WIDTH),
            buf(256, WIDTH // 2),
            buf(256, WIDTH // 2),
            buf(256, 128, dtype=jnp.int32),
            buf(256, 128, dtype=jnp.int32),
            buf(2, 256, ROWS),
            buf(2, 256, ROWS),
            dma((TA + TB,)),
            dma,
            dma,
            dma((KINDS,)),
            dma((KINDS, NC)),
            dma,
            dma,
            dma,
            dma,
            dma,
            dma,
        ],
        compiler_params=pltpu.CompilerParams(
            collective_id=0, has_side_effects=True, vmem_limit_bytes=60 << 20
        ),
        cost_estimate=pl.CostEstimate(
            flops=2 * 1024 * 1024 * 5376, bytes_accessed=12 << 20, transcendentals=1024 * 1792 // 8
        ),
        name="layer",
    )(packed_slot.reshape(1, ROWS), doc_rows, gate_weight, up_weight, down_weight)


def solution(mesh):
    return jax.shard_map(
        local,
        mesh=mesh,
        in_specs=(
            P("tensor", "dp"),
            P("tensor"),
            P("dp", "tensor"),
            P("dp", "tensor"),
            P("tensor", "dp"),
        ),
        out_specs=P("tensor", "dp"),
        check_vma=False,
    )
```

```python
import jax
import jax.numpy as jnp
from jax import lax
from jax.experimental import pallas as pl
from jax.experimental.pallas import tpu as pltpu
from jax.sharding import PartitionSpec as P

MESH = pl.DeviceIdType.MESH
BF16 = jnp.bfloat16
F32 = jnp.float32

NC = 8
TILE = 256
TA = 4
TB = 3
CA = TA * TILE
CB = TB * TILE
HB2 = CB // 2
WIDTH = 1024
ROWS = 64

A_PT, A_PL, A_CB, A_Y, B_Y, B_PT, B_PL, B_CB = (0, 0), (1, 1), (2, 1), (3, 2), (4, 3), (5, 4), (6, 5), (7, 5)
GA_Y, GA_F, GB_F, GB_Y = (8, 6), (9, 7), (10, 8), (11, 9)
T_C, T_X, X_IN, X_CORE = (12, 10), (13, 11), (14, 12), (15, 13)
GA_Z = ((16, 14), (16, 15))
GB_Z = ((17, 16), (17, 17))
KINDS = 18


ORDER = (
    0, 8, 136, 17, 19, 1, 3, 11, 24, 23, 7, 15, 18, 27, 20, 4, 12, 2, 48, 51,
    35, 10, 31, 22, 36, 28, 21, 6, 5, 14, 137, 13, 43, 44, 52, 67, 34, 26, 38, 9,
    60, 59, 42, 39, 29, 30, 46, 50, 68, 55, 47, 25, 58, 32, 53, 62, 76, 54, 37, 84,
    66, 75, 33, 83, 71, 74, 92, 70, 63, 45, 100, 78, 49, 82, 91, 41, 69, 79, 99, 90,
    61, 86, 108, 98, 57, 65, 87, 40, 94, 95, 107, 77, 116, 102, 85, 106, 103, 115, 64, 93,
    73, 81, 56, 114, 110, 101, 89, 111, 97, 118, 124, 80, 109, 72, 119, 88, 105, 122, 96, 117,
    126, 113, 128, 104, 112, 123, 125, 127,
)
DIRECT_SUM = (0,)
DIRECT_GATHER = (0,)


def kernel(
    slot_ref, doc_ref, gate_ref, up_ref, down_ref, out_ref,
    w1, wd, xs_all, pa, pb,
    pt_a, pc_a, cs_a, ys_a, yr_a,
    yr_b, q_b, pt_b, pc_b, cs_b,
    ha, hb, o2, o2r, xs, xr, acc, ysnd, yrcv,
    snd, got, pos_s, pos_g, pick_s, pick_r,
    wsem, dsem, lsem, ssem, rsem, tsend, trecv, psend, precv, gsend, grecv,
):
    dp = lax.axis_index("dp")
    t = lax.axis_index("tensor")
    z, yh = dp // 2, dp % 2
    x, yl, core = t // 4, (t // 2) % 2, t % 2
    zn, zb, z2 = (z + 1) % 4, (z + 3) % 4, (z + 2) % 4
    dev_z = ((zn * 2 + yh, t), (zb * 2 + yh, t))
    dev_z2 = (z2 * 2 + yh, t)
    dev_y = (z * 2 + 1 - yh, t)
    dev_core = (dp, t + 1 - 2 * core)
    dev_yl = (dp, t + 2 - 4 * yl)
    other = 1 - yh

    def dev_x(k):
        return (dp, ((x + k) % 4) * 4 + t % 4)

    def remote(src, dst, kind, c, device):
        return pltpu.make_async_remote_copy(
            src_ref=src, dst_ref=dst, send_sem=ssem.at[kind[0]], recv_sem=rsem.at[kind[1], c],
            device_id=device, device_id_type=MESH,
        )

    def arrive(dst, kind, c):
        remote(dst, dst, kind, c, dev_y).wait_recv()

    own_x = xs_all.at[0, pl.ds(core * ROWS, ROWS)]
    doc_load = pltpu.make_async_copy(doc_ref, own_x, lsem)
    doc_load.start()

    def w_load(h, j):
        src = (gate_ref, up_ref)[h].at[:, pl.ds(pl.multiple_of(j * TILE, TILE), TILE)]
        return pltpu.make_async_copy(src, w1.at[h, j], wsem.at[j])

    def load_tile(j, carry):
        w_load(0, j).start()
        w_load(1, j).start()
        return carry

    lax.fori_loop(0, TA + TB, load_tile, 0)
    d_load = pltpu.make_async_copy(down_ref, wd, dsem)
    d_load.start()

    barrier = pltpu.get_barrier_semaphore()

    def greet(k, carry):
        pl.semaphore_signal(
            barrier, inc=1, device_id=(dp, (t + k) % 16), device_id_type=MESH
        )
        return carry

    lax.fori_loop(1, 16, greet, 0)
    for device in (dev_z[0], dev_z[1], dev_z2, dev_y):
        pl.semaphore_signal(barrier, inc=1, device_id=device, device_id_type=MESH)
    doc_load.wait()
    pl.semaphore_wait(barrier, 19)

    remote(own_x, own_x, X_CORE, 0, dev_core).start()
    remote(own_x, xs_all.at[1, pl.ds(core * ROWS, ROWS)], X_IN, 1, dev_yl).start()

    def x_slot(k, dy):
        return 2 * k + 1 - dy

    for k in (1, 3, 2):
        c = x_slot(k, 0)
        remote(own_x, xs_all.at[c, pl.ds(core * ROWS, ROWS)], X_IN, c, dev_x(4 - k)).start()

    def plan():
        slots = slot_ref[...]
        block = lax.shift_right_logical(slots, 6)
        place = slots & 63
        blocks = lax.broadcasted_iota(jnp.int32, (16, ROWS), 0)
        hot = jnp.where(blocks == block, 1.0, 0.0)
        before = jnp.where(
            lax.broadcasted_iota(jnp.int32, (ROWS, ROWS), 0)
            < lax.broadcasted_iota(jnp.int32, (ROWS, ROWS), 1),
            1.0,
            0.0,
        )
        count = jnp.dot(hot.astype(BF16), before.astype(BF16), preferred_element_type=F32)
        rank = jnp.sum(hot * count, axis=0, keepdims=True).astype(jnp.int32)
        return block, rank, place

    def send_places():
        block, rank, place = plan()
        q = lax.broadcasted_iota(jnp.int32, (256, ROWS), 0)
        home = block * 16 + rank
        pos = 0
        for half in range(2):
            pick = home + half * 8 == q
            pick_s[half] = jnp.where(pick, 1.0, 0.0).astype(BF16)
            pos += jnp.sum(jnp.where(pick, place + 1, 0), axis=1, keepdims=True)
        pos_s[...] = jnp.broadcast_to(pos - 1, (256, 128))

        def one(k, carry):
            place_copy(k, (t + k) % 16).start()
            return carry

        lax.fori_loop(1, 16, one, 0)
        pos_g[pl.ds(t * 16, 16)] = pos_s[pl.ds(t * 16, 16)]

    def take_places():
        all_peers(pos_g, precv)
        q = lax.broadcasted_iota(jnp.int32, (256, ROWS), 0)
        here = pos_g[:, 0:ROWS] == lax.broadcasted_iota(jnp.int32, (256, ROWS), 1)
        for half in range(2):
            pick_r[half] = jnp.where(here & ((q // 8) % 2 == half), 1.0, 0.0).astype(BF16)

    def place_copy(k, peer):
        return pltpu.make_async_remote_copy(
            src_ref=pos_s.at[pl.ds(peer * 16, 16)], dst_ref=pos_g.at[pl.ds(t * 16, 16)],
            send_sem=psend, recv_sem=precv, device_id=(dp, peer), device_id_type=MESH,
        )

    def row_copy(k, peer):
        return pltpu.make_async_remote_copy(
            src_ref=snd.at[pl.ds(peer * 16, 16)], dst_ref=got.at[pl.ds(t * 16, 16)],
            send_sem=gsend, recv_sem=grecv, device_id=(dp, peer), device_id_type=MESH,
        )

    def all_peers(ref, sem):
        rows = ref.at[pl.ds(0, 240)]
        pltpu.make_async_copy(rows, rows, sem).wait()

    first = set()

    def once(name):
        new = name not in first
        first.add(name)
        return new

    def gate_up(c, dst, base, count):
        fresh = once(base)

        def tile(j, carry):
            if fresh:
                pair = w1.at[:, base + j]
                pltpu.make_async_copy(pair, pair, wsem.at[base + j]).wait()
            for h in range(2):
                r = jnp.dot(xs_all[c], w1[h, base + j], preferred_element_type=F32)
                cols = pl.ds(pl.multiple_of(j * TILE, TILE), TILE)
                dst[c, h, :, :, :, cols] = r.astype(BF16).reshape(2, 4, 16, TILE)
            return carry

        lax.fori_loop(0, count, tile, 0)

    def step_0a(c):
        arrive(xs_all.at[c, pl.ds((1 - core) * ROWS, ROWS)], X_CORE, c)
        gate_up(c, pa, 0, TA)
        for d in range(2):
            via = dev_z2 if c in DIRECT_SUM else dev_z[d]
            remote(pa.at[c, d, :, z2], pt_a.at[c, d], A_PT, c, via).start()
        for d in range(2):
            near = (zn, zb)[d]
            remote(pa.at[c, 1 - d, :, near], pc_a.at[c, 0, d], A_PL, c, dev_z[d]).start()
            if c in DIRECT_SUM:
                remote(pa.at[c, d, :, near], pc_a.at[c, 1, d], A_CB, c, dev_z[d]).start()

    def step_0b(c):
        gate_up(c, pb, TA, TB)
        remote(pb.at[c, :, other], yr_b.at[c], B_Y, c, dev_y).start()

    def next_rows(c):
        rows = xs_all.at[c, pl.ds(core * ROWS, ROWS)]
        arrive(rows, X_IN, c)
        remote(rows, rows, X_CORE, c, dev_core).start()
        if c == 1:
            for k in (1, 3, 2):
                far = x_slot(k, 1)
                remote(rows, xs_all.at[far, pl.ds(core * ROWS, ROWS)], X_IN, far, dev_x(4 - k)).start()

    def step_1a(c):
        arrive(pt_a.at[c], A_PT, c)
        if c in DIRECT_SUM:
            return
        for d in range(2):
            near = (zn, zb)[d]
            cs_a[c, d] = (pa[c, d, :, near].astype(F32) + pt_a[c, d].astype(F32)).astype(BF16)
            remote(cs_a.at[c, d], pc_a.at[c, 1, d], A_CB, c, dev_z[d]).start()

    def step_1b(c):
        arrive(yr_b.at[c], B_Y, c)
        q_b[c] = (pb[c, :, yh].astype(F32) + yr_b[c].astype(F32)).astype(BF16)
        for d in range(2):
            remote(q_b.at[c, d, z2], pt_b.at[c, d], B_PT, c, dev_z[d]).start()
        for d in range(2):
            near = (zn, zb)[d]
            remote(q_b.at[c, 1 - d, near], pc_b.at[c, 0, d], B_PL, c, dev_z[d]).start()

    def z_sum_a(c, h, y):
        total = (
            pa[c, h, y, z].astype(F32)
            + pc_a[c, 1, h, y].astype(F32)
            + pc_a[c, 0, 1 - h, y].astype(F32)
        )
        return total + pt_a[c, h, y].astype(F32) if c in DIRECT_SUM else total

    def step_2b(c):
        arrive(pt_b.at[c], B_PT, c)
        for d in range(2):
            near = (zn, zb)[d]
            cs_b[c, d] = (q_b[c, d, near].astype(F32) + pt_b[c, d].astype(F32)).astype(BF16)
            remote(cs_b.at[c, d], pc_b.at[c, 1, d], B_CB, c, dev_z[d]).start()

    def step_2a(c):
        arrive(pc_a.at[c], A_PL, c)
        for h in range(2):
            ys_a[c, h] = z_sum_a(c, h, other).astype(BF16)
        remote(ys_a.at[c], yr_a.at[c], A_Y, c, dev_y).start()

    def gated(g, u):
        return (g / (1.0 + jnp.exp(-g)) * u).astype(BF16)

    def step_3b(c):
        arrive(pc_b.at[c], B_PL, c)
        g, u = (
            q_b[c, h, z].astype(F32) + pc_b[c, 1, h].astype(F32) + pc_b[c, 0, 1 - h].astype(F32)
            for h in range(2)
        )
        hb[c, yh, z] = gated(g, u)
        for d in range(2):
            remote(hb.at[c, yh, z], hb.at[c, yh, z], GB_Z[d], c, dev_z[d]).start()
        if c in DIRECT_GATHER:
            for d in range(2):
                part = hb.at[c, yh, z, :, pl.ds(d * HB2, HB2)]
                remote(part, part, GB_F, c, dev_z2).start()

    def step_3a(c):
        arrive(yr_a.at[c], A_Y, c)
        g, u = (z_sum_a(c, h, yh) + yr_a[c, h].astype(F32) for h in range(2))
        ha[c, yh, z] = gated(g, u)
        remote(ha.at[c, yh, z], ha.at[c, yh, z], GA_Y, c, dev_y).start()

    def step_4b(c):
        for d in range(2):
            back = (zb, zn)[d]
            arrive(hb.at[c, yh, back], GB_Z[d], c)
            if c in DIRECT_GATHER:
                continue
            part = hb.at[c, yh, back, :, pl.ds(d * HB2, HB2)]
            remote(part, part, GB_F, c, dev_z[d]).start()

    def step_4a(c):
        arrive(ha.at[c, other, z], GA_Y, c)
        for d in range(2):
            remote(ha.at[c, :, z], ha.at[c, :, z], GA_Z[d], c, dev_z[d]).start()
        if c in DIRECT_GATHER:
            for d in range(2):
                remote(ha.at[c, d, z], ha.at[c, d, z], GA_F, c, dev_z2).start()

    def step_5b(c):
        arrive(hb.at[c, yh, z2], GB_F, c)
        remote(hb.at[c, yh], hb.at[c, yh], GB_Y, c, dev_y).start()

    def step_5a(c):
        for d in range(2):
            back = (zb, zn)[d]
            arrive(ha.at[c, :, back], GA_Z[d], c)
            if c in DIRECT_GATHER:
                continue
            part = ha.at[c, d, back]
            remote(part, part, GA_F, c, dev_z[d]).start()

    def step_6(c):
        arrive(ha.at[c, :, z2], GA_F, c)
        arrive(hb.at[c, other], GB_Y, c)
        if once("down"):
            d_load.wait()

        def tile(n, carry):
            cols = pl.ds(pl.multiple_of(n * TILE, TILE), TILE)
            r = jnp.dot(ha[c].reshape(128, CA), wd[0:CA, cols], preferred_element_type=F32)
            r += jnp.dot(hb[c].reshape(128, CB), wd[CA : CA + CB, cols], preferred_element_type=F32)
            o2[c, :, :, cols] = r.astype(BF16).reshape(2, ROWS, TILE)
            return carry

        lax.fori_loop(0, WIDTH // TILE, tile, 0)
        remote(o2.at[c, 1 - core], o2r.at[c], T_C, c, dev_core).start()

    def add(dy, value):
        acc[dy] = value if once(("acc", dy)) else acc[dy] + value

    def step_7(c):
        arrive(o2r.at[c], T_C, c)
        total = o2[c, core].astype(F32) + o2r[c].astype(F32)
        if c < 2:
            add(c, total)
        else:
            xs[c] = total.astype(BF16)
            remote(xs.at[c], xr.at[c], T_X, c, dev_x(c // 2)).start()

    def step_8(c):
        arrive(xr.at[c], T_X, c)
        add((c + 1) % 2, xr[c].astype(F32))

    def yl_copy():
        return pltpu.make_async_remote_copy(
            src_ref=ysnd, dst_ref=yrcv, send_sem=tsend, recv_sem=trecv, device_id=dev_yl, device_id_type=MESH
        )

    def step_y(c):
        ysnd[...] = acc[1].astype(BF16)
        yl_copy().start()

    def step_p(c):
        send_places() if c == 0 else take_places()

    steps = (
        step_0a, step_0b, next_rows, step_1a, step_1b, step_2b, step_2a, step_3b, step_3a,
        step_4b, step_4a, step_5b, step_5a, step_6, step_7, step_8, step_y, step_p,
    )
    for entry in ORDER:
        steps[entry // 8](entry % 8)

    yl_copy().wait_recv()
    rows = (
        xs_all[0, pl.ds(core * ROWS, ROWS)].astype(F32)
        + acc[0]
        + yrcv[...].astype(F32)
    ).astype(BF16)
    half = WIDTH // 2
    packed = jnp.dot(pick_s[0], rows[:, :half], preferred_element_type=F32)
    packed += jnp.dot(pick_s[1], rows[:, half:], preferred_element_type=F32)
    snd[...] = packed.astype(BF16)

    def start_rows(i, carry):
        k = (i + 6) % 15 + 1
        row_copy(k, (t + k) % 16).start()
        return carry

    lax.fori_loop(1, 16, start_rows, 0)
    got[pl.ds(t * 16, 16)] = snd[pl.ds(t * 16, 16)]

    def sent(ref, sem):
        pltpu.make_async_copy(ref, ref, sem).wait()

    sent(pt_a, ssem.at[A_PT[0]])
    sent(pc_a.at[:, 0], ssem.at[A_PL[0]])
    sent(pc_a.at[:, 1], ssem.at[A_CB[0]])
    sent(pt_b, ssem.at[B_PT[0]])
    sent(pc_b.at[:, 0], ssem.at[B_PL[0]])
    sent(pc_b.at[:, 1], ssem.at[B_CB[0]])
    sent(ha.at[:, :, pl.ds(0, 2)], ssem.at[GA_Z[0][0]])
    sent(ha.at[:, :, 0], ssem.at[GA_F[0]])
    sent(hb.at[:, 0, pl.ds(0, 2)], ssem.at[GB_Z[0][0]])
    sent(hb.at[:, 0, 0], ssem.at[GB_F[0]])
    sent(yr_a, ssem.at[A_Y[0]])
    sent(yr_b, ssem.at[B_Y[0]])
    sent(ha.at[:, 0, 0], ssem.at[GA_Y[0]])
    sent(hb.at[:, 0], ssem.at[GB_Y[0]])
    sent(o2r, ssem.at[T_C[0]])
    sent(xr.at[pl.ds(2, NC - 2)], ssem.at[T_X[0]])
    sent(xs_all.at[:, pl.ds(0, ROWS)], ssem.at[X_CORE[0]])
    sent(xs_all.at[pl.ds(1, NC - 1), pl.ds(0, ROWS)], ssem.at[X_IN[0]])
    yl_copy().wait_send()

    all_peers(pos_s, psend)
    all_peers(got, grecv)
    for part in range(2):
        out = lax.dot_general(
            pick_r[part], got[...], (((0,), (0,)), ((), ())), preferred_element_type=F32
        )
        out_ref[:, part * half : (part + 1) * half] = out.astype(BF16)

    all_peers(snd, gsend)


def local(doc_rows, packed_slot, gate_weight, up_weight, down_weight):
    anywhere = pl.BlockSpec(memory_space=pl.ANY)
    vmem = pl.BlockSpec(memory_space=pltpu.VMEM)

    def buf(*shape, dtype=BF16):
        return pltpu.VMEM(shape, dtype)

    dma = pltpu.SemaphoreType.DMA
    return pl.pallas_call(
        kernel,
        out_shape=jax.ShapeDtypeStruct((ROWS, WIDTH), BF16),
        in_specs=[vmem, anywhere, anywhere, anywhere, anywhere],
        out_specs=vmem,
        scratch_shapes=[
            buf(2, TA + TB, WIDTH, TILE),
            buf(CA + CB, WIDTH),
            buf(NC, 128, WIDTH),
            buf(NC, 2, 2, 4, 16, CA),
            buf(NC, 2, 2, 4, 16, CB),
            buf(NC, 2, 2, 16, CA),
            buf(NC, 2, 2, 2, 16, CA),
            buf(NC, 2, 2, 16, CA),
            buf(NC, 2, 16, CA),
            buf(NC, 2, 16, CA),
            buf(NC, 2, 4, 16, CB),
            buf(NC, 2, 4, 16, CB),
            buf(NC, 2, 16, CB),
            buf(NC, 2, 2, 16, CB),
            buf(NC, 2, 16, CB),
            buf(NC, 2, 4, 16, CA),
            buf(NC, 2, 4, 16, CB),
            buf(NC, 2, ROWS, WIDTH),
            buf(NC, ROWS, WIDTH),
            buf(NC, ROWS, WIDTH),
            buf(NC, ROWS, WIDTH),
            buf(2, ROWS, WIDTH, dtype=F32),
            buf(ROWS, WIDTH),
            buf(ROWS, WIDTH),
            buf(256, WIDTH // 2),
            buf(256, WIDTH // 2),
            buf(256, 128, dtype=jnp.int32),
            buf(256, 128, dtype=jnp.int32),
            buf(2, 256, ROWS),
            buf(2, 256, ROWS),
            dma((TA + TB,)),
            dma,
            dma,
            dma((KINDS,)),
            dma((KINDS, NC)),
            dma,
            dma,
            dma,
            dma,
            dma,
            dma,
        ],
        compiler_params=pltpu.CompilerParams(
            collective_id=0, has_side_effects=True, vmem_limit_bytes=55040 << 10
        ),
        cost_estimate=pl.CostEstimate(
            flops=2 * 1024 * 1024 * 5376, bytes_accessed=12 << 20, transcendentals=1024 * 1792 // 8
        ),
        name="layer",
    )(packed_slot.reshape(1, ROWS), doc_rows, gate_weight, up_weight, down_weight)


def solution(mesh):
    return jax.shard_map(
        local,
        mesh=mesh,
        in_specs=(
            P("tensor", "dp"),
            P("tensor"),
            P("dp", "tensor"),
            P("dp", "tensor"),
            P("tensor", "dp"),
        ),
        out_specs=P("tensor", "dp"),
        check_vma=False,
    )
```

```python
import jax
import jax.numpy as jnp
from jax import lax
from jax.experimental import pallas as pl
from jax.experimental.pallas import tpu as pltpu
from jax.sharding import PartitionSpec as P

MESH = pl.DeviceIdType.MESH
BF16 = jnp.bfloat16
F32 = jnp.float32

NC = 8
TILE = 256
TA = 4
TB = 3
CA = TA * TILE
CB = TB * TILE
HB2 = CB // 2
WIDTH = 1024
ROWS = 64

A_PT, A_PL, A_CB, A_Y, B_Y, B_PT, B_PL, B_CB = (0, 0), (1, 1), (2, 1), (3, 2), (4, 3), (5, 4), (6, 5), (7, 5)
GA_Y, GA_F, GB_F, GB_Y = (8, 6), (9, 7), (10, 8), (11, 9)
T_C, T_X, X_IN, X_CORE = (12, 10), (13, 11), (14, 12), (15, 13)
GA_Z, GB_Z = (16, 14), (17, 15)
KINDS = 18


ORDER = (
    0, 8, 136, 17, 19, 1, 3, 11, 24, 23, 7, 15, 18, 27, 20, 4, 12, 2, 48, 51,
    35, 10, 31, 22, 36, 28, 21, 6, 5, 14, 137, 13, 43, 44, 52, 67, 34, 26, 38, 9,
    60, 59, 42, 39, 29, 30, 46, 50, 68, 55, 47, 25, 58, 32, 53, 62, 76, 54, 37, 84,
    66, 75, 33, 83, 71, 74, 92, 70, 63, 45, 100, 78, 49, 82, 91, 41, 69, 79, 99, 90,
    61, 86, 108, 98, 57, 65, 87, 40, 94, 95, 107, 77, 116, 102, 85, 106, 103, 115, 64, 93,
    73, 81, 56, 114, 110, 101, 89, 111, 97, 118, 124, 80, 109, 72, 119, 88, 105, 122, 96, 117,
    126, 113, 128, 104, 112, 123, 125, 127,
)
DIRECT_SUM = (0,)
DIRECT_GATHER = (0,)


def kernel(
    slot_ref, doc_ref, gate_ref, up_ref, down_ref, out_ref,
    w1, wd, xs_all, pa, pb,
    pt_a, pc_a, cs_a, ys_a, yr_a,
    yr_b, q_b, pt_b, pc_b, cs_b,
    ha, hb, o2, o2r, xs, xr, acc, ysnd, yrcv,
    snd, got, pos_s, pos_g, pick_s, pick_r,
    wsem, dsem, lsem, ssem, rsem, tsend, trecv, psend, precv, gsend, grecv,
):
    dp = lax.axis_index("dp")
    t = lax.axis_index("tensor")
    z, yh = dp // 2, dp % 2
    x, yl, core = t // 4, (t // 2) % 2, t % 2
    zn, zb, z2 = (z + 1) % 4, (z + 3) % 4, (z + 2) % 4
    dev_z = ((zn * 2 + yh, t), (zb * 2 + yh, t))
    dev_z2 = (z2 * 2 + yh, t)
    dev_y = (z * 2 + 1 - yh, t)
    dev_core = (dp, t + 1 - 2 * core)
    dev_yl = (dp, t + 2 - 4 * yl)
    other = 1 - yh

    def dev_x(k):
        return (dp, ((x + k) % 4) * 4 + t % 4)

    def remote(src, dst, kind, c, device):
        return pltpu.make_async_remote_copy(
            src_ref=src, dst_ref=dst, send_sem=ssem.at[kind[0]], recv_sem=rsem.at[kind[1], c],
            device_id=device, device_id_type=MESH,
        )

    def arrive(dst, kind, c):
        remote(dst, dst, kind, c, dev_y).wait_recv()

    own_x = xs_all.at[0, pl.ds(core * ROWS, ROWS)]
    doc_load = pltpu.make_async_copy(doc_ref, own_x, lsem)
    doc_load.start()

    def w_load(h, j):
        src = (gate_ref, up_ref)[h].at[:, pl.ds(pl.multiple_of(j * TILE, TILE), TILE)]
        return pltpu.make_async_copy(src, w1.at[h, j], wsem.at[j])

    def load_tile(j, carry):
        w_load(0, j).start()
        w_load(1, j).start()
        return carry

    lax.fori_loop(0, TA + TB, load_tile, 0)
    d_load = pltpu.make_async_copy(down_ref, wd, dsem)
    d_load.start()

    barrier = pltpu.get_barrier_semaphore()

    def greet(k, carry):
        pl.semaphore_signal(
            barrier, inc=1, device_id=(dp, (t + k) % 16), device_id_type=MESH
        )
        return carry

    lax.fori_loop(1, 16, greet, 0)
    for device in (dev_z[0], dev_z[1], dev_z2, dev_y):
        pl.semaphore_signal(barrier, inc=1, device_id=device, device_id_type=MESH)
    doc_load.wait()
    pl.semaphore_wait(barrier, 19)

    remote(own_x, own_x, X_CORE, 0, dev_core).start()
    remote(own_x, xs_all.at[1, pl.ds(core * ROWS, ROWS)], X_IN, 1, dev_yl).start()

    def x_slot(k, dy):
        return 2 * k + 1 - dy

    for k in (1, 3, 2):
        c = x_slot(k, 0)
        remote(own_x, xs_all.at[c, pl.ds(core * ROWS, ROWS)], X_IN, c, dev_x(4 - k)).start()

    def plan():
        slots = slot_ref[...]
        block = lax.shift_right_logical(slots, 6)
        place = slots & 63
        blocks = lax.broadcasted_iota(jnp.int32, (16, ROWS), 0)
        hot = jnp.where(blocks == block, 1.0, 0.0)
        before = jnp.where(
            lax.broadcasted_iota(jnp.int32, (ROWS, ROWS), 0)
            < lax.broadcasted_iota(jnp.int32, (ROWS, ROWS), 1),
            1.0,
            0.0,
        )
        count = jnp.dot(hot.astype(BF16), before.astype(BF16), preferred_element_type=F32)
        rank = jnp.sum(hot * count, axis=0, keepdims=True).astype(jnp.int32)
        return block, rank, place

    def send_places():
        block, rank, place = plan()
        q = lax.broadcasted_iota(jnp.int32, (256, ROWS), 0)
        home = block * 16 + rank
        pos = 0
        for half in range(2):
            pick = home + half * 8 == q
            pick_s[half] = jnp.where(pick, 1.0, 0.0).astype(BF16)
            pos += jnp.sum(jnp.where(pick, place + 1, 0), axis=1, keepdims=True)
        pos_s[...] = jnp.broadcast_to(pos - 1, (256, 128))

        def one(k, carry):
            place_copy(k, (t + k) % 16).start()
            return carry

        lax.fori_loop(1, 16, one, 0)
        pos_g[pl.ds(t * 16, 16)] = pos_s[pl.ds(t * 16, 16)]

    def take_places():
        all_peers(pos_g, precv)
        q = lax.broadcasted_iota(jnp.int32, (256, 128), 0)
        here = pos_g[...] == lax.broadcasted_iota(jnp.int32, (256, 128), 1)
        for half in range(2):
            pick = jnp.where(here & ((q // 8) % 2 == half), 1.0, 0.0)
            pick_r[half] = pick.T[0:ROWS].astype(BF16)

    def place_copy(k, peer):
        return pltpu.make_async_remote_copy(
            src_ref=pos_s.at[pl.ds(peer * 16, 16)], dst_ref=pos_g.at[pl.ds(t * 16, 16)],
            send_sem=psend, recv_sem=precv, device_id=(dp, peer), device_id_type=MESH,
        )

    def row_copy(k, peer):
        return pltpu.make_async_remote_copy(
            src_ref=snd.at[pl.ds(peer * 16, 16)], dst_ref=got.at[pl.ds(t * 16, 16)],
            send_sem=gsend, recv_sem=grecv, device_id=(dp, peer), device_id_type=MESH,
        )

    def all_peers(ref, sem):
        rows = ref.at[pl.ds(0, 240)]
        pltpu.make_async_copy(rows, rows, sem).wait()

    first = set()

    def once(name):
        new = name not in first
        first.add(name)
        return new

    def gate_up(c, dst, base, count):
        fresh = once(base)

        def tile(j, carry):
            if fresh:
                pair = w1.at[:, base + j]
                pltpu.make_async_copy(pair, pair, wsem.at[base + j]).wait()
            for h in range(2):
                r = jnp.dot(xs_all[c], w1[h, base + j], preferred_element_type=F32)
                cols = pl.ds(pl.multiple_of(j * TILE, TILE), TILE)
                dst[c, h, :, :, :, cols] = r.astype(BF16).reshape(2, 4, 16, TILE)
            return carry

        lax.fori_loop(0, count, tile, 0)

    def step_0a(c):
        arrive(xs_all.at[c, pl.ds((1 - core) * ROWS, ROWS)], X_CORE, c)
        gate_up(c, pa, 0, TA)
        for d in range(2):
            via = dev_z2 if c in DIRECT_SUM else dev_z[d]
            remote(pa.at[c, d, :, z2], pt_a.at[c, d], A_PT, c, via).start()
        for d in range(2):
            near = (zn, zb)[d]
            remote(pa.at[c, 1 - d, :, near], pc_a.at[c, 0, d], A_PL, c, dev_z[d]).start()
            if c in DIRECT_SUM:
                remote(pa.at[c, d, :, near], pc_a.at[c, 1, d], A_CB, c, dev_z[d]).start()

    def step_0b(c):
        gate_up(c, pb, TA, TB)
        remote(pb.at[c, :, other], yr_b.at[c], B_Y, c, dev_y).start()

    def next_rows(c):
        rows = xs_all.at[c, pl.ds(core * ROWS, ROWS)]
        arrive(rows, X_IN, c)
        remote(rows, rows, X_CORE, c, dev_core).start()
        if c == 1:
            for k in (1, 3, 2):
                far = x_slot(k, 1)
                remote(rows, xs_all.at[far, pl.ds(core * ROWS, ROWS)], X_IN, far, dev_x(4 - k)).start()

    def step_1a(c):
        arrive(pt_a.at[c], A_PT, c)
        if c in DIRECT_SUM:
            return
        for d in range(2):
            near = (zn, zb)[d]
            cs_a[c, d] = (pa[c, d, :, near].astype(F32) + pt_a[c, d].astype(F32)).astype(BF16)
            remote(cs_a.at[c, d], pc_a.at[c, 1, d], A_CB, c, dev_z[d]).start()

    def step_1b(c):
        arrive(yr_b.at[c], B_Y, c)
        q_b[c] = (pb[c, :, yh].astype(F32) + yr_b[c].astype(F32)).astype(BF16)
        for d in range(2):
            remote(q_b.at[c, d, z2], pt_b.at[c, d], B_PT, c, dev_z[d]).start()
        for d in range(2):
            near = (zn, zb)[d]
            remote(q_b.at[c, 1 - d, near], pc_b.at[c, 0, d], B_PL, c, dev_z[d]).start()

    def z_sum_a(c, h, y):
        total = (
            pa[c, h, y, z].astype(F32)
            + pc_a[c, 1, h, y].astype(F32)
            + pc_a[c, 0, 1 - h, y].astype(F32)
        )
        return total + pt_a[c, h, y].astype(F32) if c in DIRECT_SUM else total

    def step_2b(c):
        arrive(pt_b.at[c], B_PT, c)
        for d in range(2):
            near = (zn, zb)[d]
            cs_b[c, d] = (q_b[c, d, near].astype(F32) + pt_b[c, d].astype(F32)).astype(BF16)
            remote(cs_b.at[c, d], pc_b.at[c, 1, d], B_CB, c, dev_z[d]).start()

    def step_2a(c):
        arrive(pc_a.at[c], A_PL, c)
        for h in range(2):
            ys_a[c, h] = z_sum_a(c, h, other).astype(BF16)
        remote(ys_a.at[c], yr_a.at[c], A_Y, c, dev_y).start()

    def gated(g, u):
        return (g / (1.0 + jnp.exp(-g)) * u).astype(BF16)

    def step_3b(c):
        arrive(pc_b.at[c], B_PL, c)
        g, u = (
            q_b[c, h, z].astype(F32) + pc_b[c, 1, h].astype(F32) + pc_b[c, 0, 1 - h].astype(F32)
            for h in range(2)
        )
        hb[c, yh, z] = gated(g, u)
        for d in range(2):
            remote(hb.at[c, yh, z], hb.at[c, yh, z], GB_Z, c, dev_z[d]).start()
        if c in DIRECT_GATHER:
            for d in range(2):
                part = hb.at[c, yh, z, :, pl.ds(d * HB2, HB2)]
                remote(part, part, GB_F, c, dev_z2).start()

    def step_3a(c):
        arrive(yr_a.at[c], A_Y, c)
        g, u = (z_sum_a(c, h, yh) + yr_a[c, h].astype(F32) for h in range(2))
        ha[c, yh, z] = gated(g, u)
        remote(ha.at[c, yh, z], ha.at[c, yh, z], GA_Y, c, dev_y).start()

    def step_4b(c):
        for d in range(2):
            back = (zb, zn)[d]
            if d == 0:
                arrive(hb.at[c, yh, pl.ds(0, 2)], GB_Z, c)
            if c in DIRECT_GATHER:
                continue
            part = hb.at[c, yh, back, :, pl.ds(d * HB2, HB2)]
            remote(part, part, GB_F, c, dev_z[d]).start()

    def step_4a(c):
        arrive(ha.at[c, other, z], GA_Y, c)
        for d in range(2):
            remote(ha.at[c, :, z], ha.at[c, :, z], GA_Z, c, dev_z[d]).start()
        if c in DIRECT_GATHER:
            for d in range(2):
                remote(ha.at[c, d, z], ha.at[c, d, z], GA_F, c, dev_z2).start()

    def step_5b(c):
        arrive(hb.at[c, yh, z2], GB_F, c)
        remote(hb.at[c, yh], hb.at[c, yh], GB_Y, c, dev_y).start()

    def step_5a(c):
        for d in range(2):
            back = (zb, zn)[d]
            if d == 0:
                arrive(ha.at[c, :, pl.ds(0, 2)], GA_Z, c)
            if c in DIRECT_GATHER:
                continue
            part = ha.at[c, d, back]
            remote(part, part, GA_F, c, dev_z[d]).start()

    def step_6(c):
        arrive(ha.at[c, :, z2], GA_F, c)
        arrive(hb.at[c, other], GB_Y, c)
        if once("down"):
            d_load.wait()

        def tile(n, carry):
            cols = pl.ds(pl.multiple_of(n * TILE, TILE), TILE)
            r = jnp.dot(ha[c].reshape(128, CA), wd[0:CA, cols], preferred_element_type=F32)
            r += jnp.dot(hb[c].reshape(128, CB), wd[CA : CA + CB, cols], preferred_element_type=F32)
            o2[c, :, :, cols] = r.astype(BF16).reshape(2, ROWS, TILE)
            return carry

        lax.fori_loop(0, WIDTH // TILE, tile, 0)
        remote(o2.at[c, 1 - core], o2r.at[c], T_C, c, dev_core).start()

    def add(dy, value):
        acc[dy] = value if once(("acc", dy)) else acc[dy] + value

    def step_7(c):
        arrive(o2r.at[c], T_C, c)
        total = o2[c, core].astype(F32) + o2r[c].astype(F32)
        if c < 2:
            add(c, total)
        else:
            xs[c] = total.astype(BF16)
            remote(xs.at[c], xr.at[c], T_X, c, dev_x(c // 2)).start()

    def step_8(c):
        arrive(xr.at[c], T_X, c)
        add((c + 1) % 2, xr[c].astype(F32))

    def yl_copy():
        return pltpu.make_async_remote_copy(
            src_ref=ysnd, dst_ref=yrcv, send_sem=tsend, recv_sem=trecv, device_id=dev_yl, device_id_type=MESH
        )

    def step_y(c):
        ysnd[...] = acc[1].astype(BF16)
        yl_copy().start()

    def step_p(c):
        send_places() if c == 0 else take_places()

    steps = (
        step_0a, step_0b, next_rows, step_1a, step_1b, step_2b, step_2a, step_3b, step_3a,
        step_4b, step_4a, step_5b, step_5a, step_6, step_7, step_8, step_y, step_p,
    )
    for entry in ORDER:
        steps[entry // 8](entry % 8)

    yl_copy().wait_recv()
    rows = (
        xs_all[0, pl.ds(core * ROWS, ROWS)].astype(F32)
        + acc[0]
        + yrcv[...].astype(F32)
    ).astype(BF16)
    half = WIDTH // 2
    packed = jnp.dot(pick_s[0], rows[:, :half], preferred_element_type=F32)
    packed += jnp.dot(pick_s[1], rows[:, half:], preferred_element_type=F32)
    snd[...] = packed.astype(BF16)

    def start_rows(i, carry):
        k = (i + 6) % 15 + 1
        row_copy(k, (t + k) % 16).start()
        return carry

    lax.fori_loop(1, 16, start_rows, 0)
    got[pl.ds(t * 16, 16)] = snd[pl.ds(t * 16, 16)]

    def sent(ref, sem):
        pltpu.make_async_copy(ref, ref, sem).wait()

    sent(pt_a, ssem.at[A_PT[0]])
    sent(pc_a.at[:, 0], ssem.at[A_PL[0]])
    sent(pc_a.at[:, 1], ssem.at[A_CB[0]])
    sent(pt_b, ssem.at[B_PT[0]])
    sent(pc_b.at[:, 0], ssem.at[B_PL[0]])
    sent(pc_b.at[:, 1], ssem.at[B_CB[0]])
    sent(ha.at[:, :, pl.ds(0, 2)], ssem.at[GA_Z[0]])
    sent(ha.at[:, :, 0], ssem.at[GA_F[0]])
    sent(hb.at[:, 0, pl.ds(0, 2)], ssem.at[GB_Z[0]])
    sent(hb.at[:, 0, 0], ssem.at[GB_F[0]])
    sent(yr_a, ssem.at[A_Y[0]])
    sent(yr_b, ssem.at[B_Y[0]])
    sent(ha.at[:, 0, 0], ssem.at[GA_Y[0]])
    sent(hb.at[:, 0], ssem.at[GB_Y[0]])
    sent(o2r, ssem.at[T_C[0]])
    sent(xr.at[pl.ds(2, NC - 2)], ssem.at[T_X[0]])
    sent(xs_all.at[:, pl.ds(0, ROWS)], ssem.at[X_CORE[0]])
    sent(xs_all.at[pl.ds(1, NC - 1), pl.ds(0, ROWS)], ssem.at[X_IN[0]])
    yl_copy().wait_send()

    all_peers(pos_s, psend)
    all_peers(got, grecv)
    for part in range(2):
        out = jnp.dot(pick_r[part], got[...], preferred_element_type=F32)
        out_ref[:, part * half : (part + 1) * half] = out.astype(BF16)

    all_peers(snd, gsend)


def local(doc_rows, packed_slot, gate_weight, up_weight, down_weight):
    anywhere = pl.BlockSpec(memory_space=pl.ANY)
    vmem = pl.BlockSpec(memory_space=pltpu.VMEM)

    def buf(*shape, dtype=BF16):
        return pltpu.VMEM(shape, dtype)

    dma = pltpu.SemaphoreType.DMA
    return pl.pallas_call(
        kernel,
        out_shape=jax.ShapeDtypeStruct((ROWS, WIDTH), BF16),
        in_specs=[vmem, anywhere, anywhere, anywhere, anywhere],
        out_specs=vmem,
        scratch_shapes=[
            buf(2, TA + TB, WIDTH, TILE),
            buf(CA + CB, WIDTH),
            buf(NC, 128, WIDTH),
            buf(NC, 2, 2, 4, 16, CA),
            buf(NC, 2, 2, 4, 16, CB),
            buf(NC, 2, 2, 16, CA),
            buf(NC, 2, 2, 2, 16, CA),
            buf(NC, 2, 2, 16, CA),
            buf(NC, 2, 16, CA),
            buf(NC, 2, 16, CA),
            buf(NC, 2, 4, 16, CB),
            buf(NC, 2, 4, 16, CB),
            buf(NC, 2, 16, CB),
            buf(NC, 2, 2, 16, CB),
            buf(NC, 2, 16, CB),
            buf(NC, 2, 4, 16, CA),
            buf(NC, 2, 4, 16, CB),
            buf(NC, 2, ROWS, WIDTH),
            buf(NC, ROWS, WIDTH),
            buf(NC, ROWS, WIDTH),
            buf(NC, ROWS, WIDTH),
            buf(2, ROWS, WIDTH, dtype=F32),
            buf(ROWS, WIDTH),
            buf(ROWS, WIDTH),
            buf(256, WIDTH // 2),
            buf(256, WIDTH // 2),
            buf(256, 128, dtype=jnp.int32),
            buf(256, 128, dtype=jnp.int32),
            buf(2, 256, ROWS),
            buf(2, ROWS, 256),
            dma((TA + TB,)),
            dma,
            dma,
            dma((KINDS,)),
            dma((16, NC)),
            dma,
            dma,
            dma,
            dma,
            dma,
            dma,
        ],
        compiler_params=pltpu.CompilerParams(
            collective_id=0, has_side_effects=True, vmem_limit_bytes=55040 << 10
        ),
        cost_estimate=pl.CostEstimate(
            flops=2 * 1024 * 1024 * 5376, bytes_accessed=12 << 20, transcendentals=1024 * 1792 // 8
        ),
        name="layer",
    )(packed_slot.reshape(1, ROWS), doc_rows, gate_weight, up_weight, down_weight)


def solution(mesh):
    return jax.shard_map(
        local,
        mesh=mesh,
        in_specs=(
            P("tensor", "dp"),
            P("tensor"),
            P("dp", "tensor"),
            P("dp", "tensor"),
            P("tensor", "dp"),
        ),
        out_specs=P("tensor", "dp"),
        check_vma=False,
    )
```
